32 devices in a mesh: branch: 2 (over x), sky: 16 (over z, y, core).
Axes of the slice: x: 2, y: 2, z: 4, core: 2. Of those that a mesh axis runs over, the one named last changes fastest.
Arguments:
- sky_maps: bfloat16 [2, 64, 4096], P('branch', None, 'sky'), may hold values from -6 to 6
- footprint: int32 [2, 4096], P('branch', 'sky'), may hold values 0 or 1
- neighbours: int32 [9, 4096], P(None, 'sky'), may hold values from -1 to 4095, as said below
- enc_weight: bfloat16 [2, 6, 9, 64, 64], P('branch'), may hold values from -0.1875 to 0.1875
- join_weight: bfloat16 [256, 128], P(None, 'branch'), may hold values from -0.5 to 0.5
- dec_weight: bfloat16 [9, 256, 256], P(None, 'branch'), may hold values from -0.125 to 0.125
- cotangent: bfloat16 [256, 4096], P('branch', 'sky'), may hold values from -6 to 6
Outputs:
- map_grads: bfloat16 [2, 64, 4096], P('branch', None, 'sky')
- weight_grads: float32 [2, 6, 9, 64, 64], P('branch')
The draws below stay inside these ranges and needn't reach their ends.
Inputs may be any that keep to these rules, and one draw needn't show every extreme that they name: `neighbours`: slot 4 of each row is the row itself; every other entry is -1 or a row index that differs from the row's own by at most 256.
All inputs are finite; a program needn't handle non-finite values. No bound on the sum of `footprint` on one device may be relied on, other than what follows from the above.
Results may differ from the reference program's by a relative error of at most 0.017.
Values may be sent and summed in bfloat16 or wider, within the bound.
A program may use at most 64 MiB of HBM per device.

```python
import math
import jax
import jax.numpy as jnp
from jax import lax

C = 64
FD = 256
LAYERS = 6
TAPS = 9
ROW_DEV = 256
BINS = 2
ROWS = 4096


def draw_neighbours(key, part):
    draw_key, second = jax.random.split(key)
    offsets = jax.random.randint(draw_key, (9, ROWS), -ROW_DEV, ROW_DEV + 1)
    tap_index = jnp.arange(9, dtype=jnp.int32)[:, None]
    offsets = jnp.where(tap_index == 4, 0, offsets)
    absent = jax.random.randint(second, (9, ROWS), 0, 8)
    column = jnp.arange(ROWS, dtype=jnp.int32)[None, :]
    target = column + offsets
    retained = (target >= 0) & (target < ROWS) & ((absent > 0) | (tap_index == 4))
    return jnp.where(retained, target, -1).astype(jnp.int32)


def plant(drawn, rng, smallest, largest):
    extent = drawn.shape
    index_at = [jax.random.randint(jax.random.fold_in(rng, axis), (), 0, extent[axis]) for axis in range(len(extent))]
    drawn = drawn.at[tuple(index_at)].set(smallest)
    longest = extent.index(max(extent))
    index_at[longest] = (index_at[longest] + 1) % extent[longest]
    return drawn.at[tuple(index_at)].set(largest)


def block_levels(key, shape, shards, smallest, high):
    level, own = 1.0, jax.random.fold_in(key, 6)
    for position, parts in shards:
        heights = jnp.exp(jax.random.uniform(jax.random.fold_in(own, position), (parts,), jnp.float32, smallest / len(shards), high / len(shards)))
        level = level * jnp.repeat(heights, shape[position] // parts).reshape([-1 if axis == position else 1 for axis in range(len(shape))])
    return level


def gaussian(stream_key, shape, deviation, most, pieces=(), held_as=jnp.bfloat16):
    factor_of = block_levels(stream_key, shape, pieces, -0.22, 0.18) if pieces else 1.0
    result = jax.random.normal(stream_key, shape, jnp.float32) * deviation * factor_of
    return jnp.minimum(jnp.maximum(result, -most), most).astype(held_as)


def setup_inputs(seed: int = 0) -> dict:
    seeds = jax.random.split(jax.random.key(seed), 8)
    sky_maps = gaussian(seeds[0], (BINS, C, ROWS), 1.0, 6.0, ((0, 2), (2, 16)))
    footprint = plant((jax.random.randint(seeds[1], (BINS, ROWS), 0, 4) < 3).astype(jnp.int32), jax.random.fold_in(seeds[1], 1), 0, 1)
    neighbours = draw_neighbours(jax.random.fold_in(seeds[7], 71), 0)
    enc_weight = gaussian(seeds[3], (BINS, LAYERS, TAPS, C, C), (18 * C) ** -0.5, 0.1875, ((0, 2),))
    join_weight = gaussian(seeds[4], (FD, BINS * C), (BINS * C) ** -0.5, 0.5, ((1, 2),))
    dec_weight = gaussian(seeds[5], (TAPS, FD, FD), (9 * FD) ** -0.5, 0.125, ((1, 2),))
    cotangent = gaussian(seeds[6], (FD, ROWS), 1.0, 6.0, ((0, 2), (1, 16)))
    return {"sky_maps": sky_maps, "footprint": footprint, "neighbours": neighbours, "enc_weight": enc_weight, "join_weight": join_weight, "dec_weight": dec_weight, "cotangent": cotangent}


def silu_slope(value):
    sigmoid = jax.nn.sigmoid(value)
    return sigmoid * (1.0 + value * (1.0 - sigmoid))

def reference(sky_maps, footprint, neighbours, enc_weight, join_weight, dec_weight, cotangent):
    present = neighbours >= 0
    clamped = jnp.where(present, neighbours, 0).astype(jnp.int32)
    bin_count = sky_maps.shape[0]
    channels = sky_maps.shape[1]
    row_total = sky_maps.shape[2]
    depth = enc_weight.shape[1]

    def pick(source, tap_index):
        gathered = jnp.take(source, clamped[tap_index], axis=1)
        return jnp.where(present[tap_index][None, :], gathered, jnp.zeros((), source.dtype))

    def place(target, contrib, tap_index):
        contrib = jnp.where(present[tap_index][None, :], contrib, 0.0)
        return target.at[:, clamped[tap_index]].add(contrib)
    saved_states = []
    saved_pre = []
    joining = jnp.zeros((join_weight.shape[0], row_total), jnp.float32)
    for bin_index in range(bin_count):
        retained = footprint[bin_index].astype(jnp.float32)[None, :]
        hidden = sky_maps[bin_index]
        states = []
        pres = []
        for layer_index in range(depth):
            preact = jnp.zeros((channels, row_total), jnp.float32)
            for tap_index in range(9):
                preact = preact + jnp.dot(enc_weight[bin_index, layer_index, tap_index], pick(hidden, tap_index), preferred_element_type=jnp.float32)
            states.append(hidden)
            pres.append(preact)
            hidden = (retained * (hidden.astype(jnp.float32) + jax.nn.silu(preact))).astype(jnp.bfloat16)
        saved_states.append(states)
        saved_pre.append(pres)
        joining = joining + jnp.dot(join_weight[:, bin_index * channels:(bin_index + 1) * channels], hidden, preferred_element_type=jnp.float32)
    slope = silu_slope(joining).astype(jnp.bfloat16)
    unit_acc = jnp.zeros((dec_weight.shape[2], row_total), jnp.float32)
    for tap_index in range(9):
        unit_acc = place(unit_acc, jnp.dot(dec_weight[tap_index].T, cotangent, preferred_element_type=jnp.float32), tap_index)
    unit_grad = (unit_acc * slope.astype(jnp.float32)).astype(jnp.bfloat16)
    normalizer = 1.0 / math.sqrt(row_total)
    map_list = []
    weight_list = []
    for bin_index in range(bin_count):
        retained = footprint[bin_index].astype(jnp.float32)[None, :]
        gradient = jnp.dot(join_weight[:, bin_index * channels:(bin_index + 1) * channels].T, unit_grad, preferred_element_type=jnp.float32)
        layer_grads = [None] * depth
        for layer_index in reversed(range(depth)):
            masked = retained * gradient
            act_grad = (masked * silu_slope(saved_pre[bin_index][layer_index])).astype(jnp.bfloat16)
            spread = jnp.zeros((channels, row_total), jnp.float32)
            tap_grads = []
            for tap_index in range(9):
                picked = pick(saved_states[bin_index][layer_index], tap_index)
                tap_grads.append(lax.dot_general(act_grad, picked, (((1,), (1,)), ((), ())), preferred_element_type=jnp.float32))
                spread = place(spread, jnp.dot(enc_weight[bin_index, layer_index, tap_index].T, act_grad, preferred_element_type=jnp.float32), tap_index)
            layer_grads[layer_index] = jnp.stack(tap_grads) * normalizer
            gradient = masked + spread
        map_list.append(gradient.astype(jnp.bfloat16))
        weight_list.append(jnp.stack(layer_grads))
    return (jnp.stack(map_list), jnp.stack(weight_list))
```

```python
import functools
import math

import jax
import jax.numpy as jnp
from jax import lax
from jax.experimental import pallas as pl
from jax.experimental.pallas import tpu as pltpu
from jax.sharding import PartitionSpec as P

MESH = pl.DeviceIdType.MESH
F32 = jnp.float32
BF16 = jnp.bfloat16


def matmul(a, b, contract=((1,), (0,))):
    return lax.dot_general(a, b, (contract, ((), ())), preferred_element_type=F32)


def kernel(
    n_sky, n_branch,
    maps, foot, nb, enc, join, dec, cot,
    map_out, grad_out,
    own, from_left, from_right, picked, slope, one_hot, one_hot_t, rel, enc_flat, enc_t,
    grad, edge_left, edge_right, back_left, back_right,
    dec_acc, rim_left, rim_right, got_left, got_right, unit_own, unit_send, unit_got,
    join_got, top_got,
    fwd_send, fwd_recv, bwd_send, bwd_recv, rim_send, rim_recv, br_send, br_recv,
):
    depth, taps = enc.shape[0], enc.shape[1]
    chans, rows = maps.shape
    sky = lax.axis_index("sky")
    branch = lax.axis_index("branch")
    has_left, has_right = sky > 0, sky < n_sky - 1
    left, right = jnp.maximum(sky - 1, 0), jnp.minimum(sky + 1, n_sky - 1)
    peers = [(d, lax.rem(branch + d, n_branch)) for d in range(1, n_branch)]

    barrier = pltpu.get_barrier_semaphore()

    @pl.when(has_left)
    def _():
        pl.semaphore_signal(barrier, inc=1, device_id={"sky": left}, device_id_type=MESH)

    @pl.when(has_right)
    def _():
        pl.semaphore_signal(barrier, inc=1, device_id={"sky": right}, device_id_type=MESH)

    for _, peer in peers:
        pl.semaphore_signal(barrier, inc=1, device_id={"branch": peer}, device_id_type=MESH)
    pl.semaphore_wait(
        barrier, has_left.astype(jnp.int32) + has_right.astype(jnp.int32) + (n_branch - 1)
    )

    def to_left(src, dst, send, recv):
        return pltpu.make_async_remote_copy(
            src_ref=src, dst_ref=dst, send_sem=send, recv_sem=recv,
            device_id={"sky": left}, device_id_type=MESH,
        )

    def to_right(src, dst, send, recv):
        return pltpu.make_async_remote_copy(
            src_ref=src, dst_ref=dst, send_sem=send, recv_sem=recv,
            device_id={"sky": right}, device_id_type=MESH,
        )

    def halo(layer):
        return (
            to_left(own.at[layer], from_right.at[layer], fwd_send.at[layer, 0], fwd_recv.at[layer, 0]),
            to_right(own.at[layer], from_left.at[layer], fwd_send.at[layer, 1], fwd_recv.at[layer, 1]),
        )

    def back(layer):
        return (
            to_left(edge_left.at[layer], back_right.at[layer], bwd_send.at[layer, 0], bwd_recv.at[layer, 0]),
            to_right(edge_right.at[layer], back_left.at[layer], bwd_send.at[layer, 1], bwd_recv.at[layer, 1]),
        )

    def rims():
        return (
            to_left(rim_left, got_right, rim_send.at[0], rim_recv.at[0]),
            to_right(rim_right, got_left, rim_send.at[1], rim_recv.at[1]),
        )

    def start(pair):
        @pl.when(has_left)
        def _():
            pair[0].start()

        @pl.when(has_right)
        def _():
            pair[1].start()

    def wait_recv(pair):
        @pl.when(has_right)
        def _():
            pair[0].wait_recv()

        @pl.when(has_left)
        def _():
            pair[1].wait_recv()

    def wait_send(pair):
        @pl.when(has_left)
        def _():
            pair[0].wait_send()

        @pl.when(has_right)
        def _():
            pair[1].wait_send()

    def across(src, dst, kind):
        return [
            pltpu.make_async_remote_copy(
                src_ref=src, dst_ref=dst.at[d - 1],
                send_sem=br_send.at[kind, d - 1], recv_sem=br_recv.at[kind, d - 1],
                device_id={"branch": peer}, device_id_type=MESH,
            )
            for d, peer in peers
        ]

    own[0] = maps[...]
    start(halo(0))
    join_copies = across(join, join_got, 0)
    for copy in join_copies:
        copy.start()

    @pl.when(jnp.logical_not(has_left))
    def _():
        from_left[...] = jnp.zeros_like(from_left)
        back_left[...] = jnp.zeros_like(back_left)
        got_left[...] = jnp.zeros_like(got_left)

    @pl.when(jnp.logical_not(has_right))
    def _():
        from_right[...] = jnp.zeros_like(from_right)
        back_right[...] = jnp.zeros_like(back_right)
        got_right[...] = jnp.zeros_like(got_right)

    first = (sky - 1) * rows
    near = nb[...]
    offset = jnp.where(near >= 0, near - first, -1)
    part = jnp.where(
        offset < 0, -1,
        jnp.where(offset < rows, offset + rows, jnp.where(offset < 2 * rows, offset - rows, offset)),
    )
    rel[...] = jnp.full(rel.shape, -1, jnp.int32)
    rel[0:taps, :] = part
    col = jnp.transpose(rel[...])
    for k in range(taps):
        lanes = slice(k * rows, (k + 1) * rows)
        line = rel[k : k + 1, :]
        for p in range(3):
            index = lax.broadcasted_iota(jnp.int32, (rows, rows), 0) + p * rows
            one_hot[p * rows : (p + 1) * rows, lanes] = jnp.where(line == index, 1.0, 0.0).astype(BF16)
            index = lax.broadcasted_iota(jnp.int32, (rows, rows), 1) + p * rows
            one_hot_t[lanes, p * rows : (p + 1) * rows] = jnp.where(
                col[:, k : k + 1] == index, 1.0, 0.0
            ).astype(BF16)

    retained = foot[...].astype(F32)
    dec_acc[...] = jnp.zeros_like(dec_acc)
    dec_steps = 3

    @pl.loop(0, depth)
    def forward(layer):
        hidden = own[layer]
        for k in range(taps):
            block = matmul(hidden, one_hot[0:rows, k * rows : (k + 1) * rows])
            picked[layer, k * chans : (k + 1) * chans, :] = block.astype(BF16)
        for k in range(taps):
            tap = enc[layer, k]
            enc_flat[layer, :, k * chans : (k + 1) * chans] = tap
            enc_t[layer, k * chans : (k + 1) * chans, :] = jnp.transpose(tap)

        @pl.when(layer < dec_steps)
        def _():
            each = taps // dec_steps
            parts = []
            for j in range(each):
                term = matmul(dec[layer * each + j], cot[...], ((0,), (0,)))
                parts.append(term.astype(BF16))
            span = each * rows
            table = one_hot_t[pl.ds(pl.multiple_of(layer * span, span), span), :]
            dec_acc[...] += matmul(jnp.concatenate(parts, axis=1), table)

        @pl.when(layer == dec_steps)
        def _():
            rim_left[...] = dec_acc[:, rows : 2 * rows].astype(BF16)
            rim_right[...] = dec_acc[:, 2 * rows : 3 * rows].astype(BF16)
            start(rims())

        @pl.when(layer == dec_steps + 1)
        def _():
            wait_recv(rims())
            total = dec_acc[:, 0:rows] + got_left[...].astype(F32) + got_right[...].astype(F32)
            unit_own[...] = total
            unit_send[...] = total.astype(BF16)
            for copy in across(unit_send, unit_got, 1):
                copy.start()

        wait_recv(halo(layer))
        for k in range(taps):
            lanes = slice(k * rows, (k + 1) * rows)
            both = jnp.concatenate([from_left[layer], from_right[layer]], axis=1)
            block = matmul(both, one_hot[rows : 3 * rows, lanes])
            at = slice(k * chans, (k + 1) * chans)
            picked[layer, at, :] = picked[layer, at, :] + block.astype(BF16)
        pre = matmul(enc_flat[layer], picked[layer])
        sig = jax.nn.sigmoid(pre)
        after = retained * (hidden.astype(F32) + pre * sig)
        own[layer + 1] = after.astype(BF16)

        @pl.when(layer < depth - 1)
        def _():
            start(halo(layer + 1))

        slope[layer] = sig * (1.0 + pre * (1.0 - sig))

    top_copies = across(own.at[depth], top_got, 2)
    for copy in top_copies:
        copy.start()
    joined = matmul(join[...], own[depth])
    for copy in join_copies:
        copy.wait_recv()
    unit_copies = across(unit_send, unit_got, 1)
    unit = unit_own[...]
    for i, copy in enumerate(unit_copies):
        copy.wait_recv()
        unit = unit + unit_got[i].astype(F32)
    for i, copy in enumerate(top_copies):
        copy.wait_recv()
        joined = joined + matmul(join_got[i], top_got[i])
    sig = jax.nn.sigmoid(joined)
    unit_slope = (sig * (1.0 + joined * (1.0 - sig))).astype(BF16).astype(F32)
    unit_grad = (unit * unit_slope).astype(BF16)
    grad[...] = matmul(join[...], unit_grad, ((0,), (0,)))

    @pl.loop(0, depth)
    def backward(step):
        layer = depth - 1 - step
        masked = retained * grad[...]
        act = (masked * slope[layer]).astype(BF16)
        terms = matmul(enc_t[layer], act).astype(BF16)
        terms = jnp.concatenate(
            [terms[k * chans : (k + 1) * chans] for k in range(taps)], axis=1
        )
        edge = matmul(terms, one_hot_t[:, rows : 3 * rows]).astype(BF16)
        edge_left[layer] = edge[:, :rows]
        edge_right[layer] = edge[:, rows:]
        start(back(layer))
        inner = masked + matmul(terms, one_hot_t[:, 0:rows])
        weight = matmul(act, picked[layer], ((1,), (1,)))
        for k in range(taps):
            grad_out[layer, k] = weight[:, k * chans : (k + 1) * chans]
        wait_recv(back(layer))
        grad[...] = inner + back_left[layer].astype(F32) + back_right[layer].astype(F32)

    map_out[...] = grad[...].astype(BF16)

    @pl.loop(0, depth)
    def drain(layer):
        wait_send(halo(layer))
        wait_send(back(layer))

    wait_send(rims())
    for copy in join_copies + unit_copies + top_copies:
        copy.wait_send()


def per_device(n_sky, n_branch, sky_maps, footprint, neighbours, enc_weight, join_weight, dec_weight, cotangent):
    chans, rows = sky_maps.shape[1:]
    depth, taps = enc_weight.shape[1:3]
    width = dec_weight.shape[2]
    others = max(n_branch - 1, 1)
    vmem = pltpu.VMEM
    dma = pltpu.SemaphoreType.DMA
    layers = (depth, chans, rows)
    scratch = [
        vmem((depth + 1, chans, rows), BF16),
        vmem(layers, BF16),
        vmem(layers, BF16),
        vmem((depth, taps * chans, rows), BF16),
        vmem(layers, F32),
        vmem((3 * rows, taps * rows), BF16),
        vmem((taps * rows, 3 * rows), BF16),
        vmem((128, rows), jnp.int32),
        vmem((depth, chans, taps * chans), BF16),
        vmem((depth, taps * chans, chans), BF16),
        vmem((chans, rows), F32),
        vmem(layers, BF16),
        vmem(layers, BF16),
        vmem(layers, BF16),
        vmem(layers, BF16),
        vmem((width, 3 * rows), F32),
        vmem((width, rows), BF16),
        vmem((width, rows), BF16),
        vmem((width, rows), BF16),
        vmem((width, rows), BF16),
        vmem((width, rows), F32),
        vmem((width, rows), BF16),
        vmem((others, width, rows), BF16),
        vmem((others, width, chans), BF16),
        vmem((others, chans, rows), BF16),
        dma((depth, 2)), dma((depth, 2)), dma((depth, 2)), dma((depth, 2)),
        dma((2,)), dma((2,)), dma((3, others)), dma((3, others)),
    ]
    whole = pl.BlockSpec(memory_space=pltpu.VMEM)
    map_grad, tap_grads = pl.pallas_call(
        functools.partial(kernel, n_sky, n_branch),
        out_shape=(
            jax.ShapeDtypeStruct((chans, rows), BF16),
            jax.ShapeDtypeStruct((depth, taps, chans, chans), F32),
        ),
        in_specs=[whole] * 7,
        out_specs=(whole, whole),
        scratch_shapes=scratch,
        compiler_params=pltpu.CompilerParams(
            collective_id=0, has_side_effects=True, vmem_limit_bytes=48 * 1024 * 1024
        ),
        name="unet_backward",
    )(sky_maps[0], footprint, neighbours, enc_weight[0], join_weight, dec_weight, cotangent)
    normalizer = 1.0 / math.sqrt(rows * n_sky)
    summed = lax.psum(tap_grads, "sky") * normalizer
    return map_grad[None], summed[None]


def solution(mesh):
    in_specs = (
        P("branch", None, "sky"),
        P("branch", "sky"),
        P(None, "sky"),
        P("branch", None, None, None, None),
        P(None, "branch"),
        P(None, "branch", None),
        P("branch", "sky"),
    )
    out_specs = (P("branch", None, "sky"), P("branch", None, None, None, None))
    return jax.shard_map(
        functools.partial(per_device, mesh.shape["sky"], mesh.shape["branch"]),
        mesh=mesh, in_specs=in_specs, out_specs=out_specs, check_vma=False,
    )
```

```python
import functools
import math

import jax
import jax.numpy as jnp
from jax import lax
from jax.experimental import pallas as pl
from jax.experimental.pallas import tpu as pltpu
from jax.sharding import PartitionSpec as P

MESH = pl.DeviceIdType.MESH
F32 = jnp.float32
BF16 = jnp.bfloat16


def matmul(a, b, contract=((1,), (0,))):
    return lax.dot_general(a, b, (contract, ((), ())), preferred_element_type=F32)


def kernel(
    n_sky, n_branch, near_group,
    maps_in, foot_in, nb_in, enc_in, join_in, dec_in, cot_in,
    map_out, grad_out,
    foot, nb, enc, join, dec, cot,
    own, from_left, from_right, picked, slope, one_hot, one_hot_t, rel, enc_flat, enc_t,
    grad, edge_left, edge_right, back_left, back_right,
    dec_acc, rim_left, rim_right, got_left, got_right, unit_own, unit_send, unit_got,
    join_got, top_got,
    part_own, part_got, mid, final,
    fwd_send, fwd_recv, bwd_send, bwd_recv, rim_send, rim_recv, br_send, br_recv,
    near_send, near_recv, far_send, far_recv, out_send, out_recv, local_sem,
):
    depth, taps = enc.shape[0], enc.shape[1]
    chans, rows = maps_in.shape
    far_group = n_sky // near_group
    share = chans // near_group
    sky = lax.axis_index("sky")
    branch = lax.axis_index("branch")
    has_left, has_right = sky > 0, sky < n_sky - 1
    left, right = jnp.maximum(sky - 1, 0), jnp.minimum(sky + 1, n_sky - 1)
    peers = [(d, lax.rem(branch + d, n_branch)) for d in range(1, n_branch)]

    mine = lax.rem(sky, near_group)
    level = sky // near_group
    mates = [
        (d, sky - mine + lax.rem(mine + d, near_group)) for d in range(1, near_group)
    ]
    stack = [
        (d, lax.rem(level + d, far_group) * near_group + mine) for d in range(1, far_group)
    ]

    sources = (maps_in, foot_in, nb_in, join_in, enc_in, dec_in, cot_in)
    targets = (own.at[0], foot, nb, join, enc, dec, cot)
    loads = [
        pltpu.make_async_copy(src, dst, local_sem.at[i])
        for i, (src, dst) in enumerate(zip(sources, targets))
    ]
    for load in loads:
        load.start()

    barrier = pltpu.get_barrier_semaphore()

    @pl.when(has_left)
    def _():
        pl.semaphore_signal(barrier, inc=1, device_id={"sky": left}, device_id_type=MESH)

    @pl.when(has_right)
    def _():
        pl.semaphore_signal(barrier, inc=1, device_id={"sky": right}, device_id_type=MESH)

    for _, peer in peers:
        pl.semaphore_signal(barrier, inc=1, device_id={"branch": peer}, device_id_type=MESH)
    for _, peer in mates + stack:
        pl.semaphore_signal(barrier, inc=1, device_id={"sky": peer}, device_id_type=MESH)
    pl.semaphore_wait(
        barrier,
        has_left.astype(jnp.int32) + has_right.astype(jnp.int32)
        + (n_branch - 1 + near_group - 1 + far_group - 1),
    )

    def to_left(src, dst, send, recv):
        return pltpu.make_async_remote_copy(
            src_ref=src, dst_ref=dst, send_sem=send, recv_sem=recv,
            device_id={"sky": left}, device_id_type=MESH,
        )

    def to_right(src, dst, send, recv):
        return pltpu.make_async_remote_copy(
            src_ref=src, dst_ref=dst, send_sem=send, recv_sem=recv,
            device_id={"sky": right}, device_id_type=MESH,
        )

    def halo(layer):
        return (
            to_left(own.at[layer], from_right.at[layer], fwd_send.at[layer, 0], fwd_recv.at[layer, 0]),
            to_right(own.at[layer], from_left.at[layer], fwd_send.at[layer, 1], fwd_recv.at[layer, 1]),
        )

    def back(layer):
        return (
            to_left(edge_left.at[layer], back_right.at[layer], bwd_send.at[layer, 0], bwd_recv.at[layer, 0]),
            to_right(edge_right.at[layer], back_left.at[layer], bwd_send.at[layer, 1], bwd_recv.at[layer, 1]),
        )

    def rims():
        return (
            to_left(rim_left, got_right, rim_send.at[0], rim_recv.at[0]),
            to_right(rim_right, got_left, rim_send.at[1], rim_recv.at[1]),
        )

    def start(pair):
        @pl.when(has_left)
        def _():
            pair[0].start()

        @pl.when(has_right)
        def _():
            pair[1].start()

    def wait_recv(pair):
        @pl.when(has_right)
        def _():
            pair[0].wait_recv()

        @pl.when(has_left)
        def _():
            pair[1].wait_recv()

    def wait_send(pair):
        @pl.when(has_left)
        def _():
            pair[0].wait_send()

        @pl.when(has_right)
        def _():
            pair[1].wait_send()

    def across(src, dst, kind):
        return [
            pltpu.make_async_remote_copy(
                src_ref=src, dst_ref=dst.at[d - 1],
                send_sem=br_send.at[kind, d - 1], recv_sem=br_recv.at[kind, d - 1],
                device_id={"branch": peer}, device_id_type=MESH,
            )
            for d, peer in peers
        ]

    def over_sky(peer, src, dst, send, recv):
        return pltpu.make_async_remote_copy(
            src_ref=src, dst_ref=dst, send_sem=send, recv_sem=recv,
            device_id={"sky": peer}, device_id_type=MESH,
        )

    def scatter_copies(layer):
        return [
            over_sky(
                peer, part_own.at[layer, lax.rem(mine + d, near_group)], part_got.at[layer, d - 1],
                near_send.at[layer, d - 1], near_recv.at[layer, d - 1],
            )
            for d, peer in mates
        ]

    def level_copies(layer):
        return [
            over_sky(
                peer, mid.at[layer, level], mid.at[layer, level],
                far_send.at[layer, d - 1], far_recv.at[layer, d - 1],
            )
            for d, peer in stack
        ]

    def gather_copies(layer):
        return [
            over_sky(
                peer, final.at[layer, mine], final.at[layer, mine],
                out_send.at[layer, d - 1], out_recv.at[layer, d - 1],
            )
            for d, peer in mates
        ]

    def sum_near(layer):
        total = part_own[layer, mine].astype(F32)
        for i, copy in enumerate(scatter_copies(layer)):
            copy.wait_recv()
            total = total + part_got[layer, i].astype(F32)
        mid[layer, level] = total.astype(BF16)
        for copy in level_copies(layer):
            copy.start()

    def sum_far(layer):
        for copy in level_copies(layer):
            copy.wait_recv()
        total = mid[layer, 0].astype(F32)
        for z in range(1, far_group):
            total = total + mid[layer, z].astype(F32)
        final[layer, mine] = total.astype(BF16)
        for copy in gather_copies(layer):
            copy.start()

    def finish(layer):
        for copy in gather_copies(layer):
            copy.wait_recv()
        whole = jnp.concatenate([final[layer, i] for i in range(near_group)], axis=0)
        for k in range(taps):
            grad_out[layer, k] = whole[:, k * chans : (k + 1) * chans]

    loads[0].wait()
    start(halo(0))
    loads[3].wait()
    join_copies = across(join, join_got, 0)
    for copy in join_copies:
        copy.start()

    @pl.when(jnp.logical_not(has_left))
    def _():
        from_left[...] = jnp.zeros_like(from_left)
        back_left[...] = jnp.zeros_like(back_left)
        got_left[...] = jnp.zeros_like(got_left)

    @pl.when(jnp.logical_not(has_right))
    def _():
        from_right[...] = jnp.zeros_like(from_right)
        back_right[...] = jnp.zeros_like(back_right)
        got_right[...] = jnp.zeros_like(got_right)

    loads[1].wait()
    loads[2].wait()
    first = (sky - 1) * rows
    near = nb[...]
    offset = jnp.where(near >= 0, near - first, -1)
    part = jnp.where(
        offset < 0, -1,
        jnp.where(offset < rows, offset + rows, jnp.where(offset < 2 * rows, offset - rows, offset)),
    )
    rel[...] = jnp.full(rel.shape, -1, jnp.int32)
    rel[0:taps, :] = part
    col = jnp.transpose(rel[...])
    for k in range(taps):
        lanes = slice(k * rows, (k + 1) * rows)
        line = rel[k : k + 1, :]
        for p in range(3):
            index = lax.broadcasted_iota(jnp.int32, (rows, rows), 0) + p * rows
            one_hot[p * rows : (p + 1) * rows, lanes] = jnp.where(line == index, 1.0, 0.0).astype(BF16)
            index = lax.broadcasted_iota(jnp.int32, (rows, rows), 1) + p * rows
            one_hot_t[lanes, p * rows : (p + 1) * rows] = jnp.where(
                col[:, k : k + 1] == index, 1.0, 0.0
            ).astype(BF16)

    for load in loads[4:]:
        load.wait()
    retained = foot[...].astype(F32)
    dec_acc[...] = jnp.zeros_like(dec_acc)
    dec_steps = 3

    @pl.loop(0, depth)
    def forward(layer):
        hidden = own[layer]
        for k in range(taps):
            block = matmul(hidden, one_hot[0:rows, k * rows : (k + 1) * rows])
            picked[layer, k * chans : (k + 1) * chans, :] = block.astype(BF16)
        for k in range(taps):
            tap = enc[layer, k]
            enc_flat[layer, :, k * chans : (k + 1) * chans] = tap
            enc_t[layer, k * chans : (k + 1) * chans, :] = jnp.transpose(tap)

        @pl.when(layer < dec_steps)
        def _():
            each = taps // dec_steps
            parts = []
            for j in range(each):
                term = matmul(dec[layer * each + j], cot[...], ((0,), (0,)))
                parts.append(term.astype(BF16))
            span = each * rows
            table = one_hot_t[pl.ds(pl.multiple_of(layer * span, span), span), :]
            dec_acc[...] += matmul(jnp.concatenate(parts, axis=1), table)

        @pl.when(layer == dec_steps)
        def _():
            rim_left[...] = dec_acc[:, rows : 2 * rows].astype(BF16)
            rim_right[...] = dec_acc[:, 2 * rows : 3 * rows].astype(BF16)
            start(rims())

        @pl.when(layer == dec_steps + 1)
        def _():
            wait_recv(rims())
            total = dec_acc[:, 0:rows] + got_left[...].astype(F32) + got_right[...].astype(F32)
            unit_own[...] = total
            unit_send[...] = total.astype(BF16)
            for copy in across(unit_send, unit_got, 1):
                copy.start()

        wait_recv(halo(layer))
        for k in range(taps):
            lanes = slice(k * rows, (k + 1) * rows)
            both = jnp.concatenate([from_left[layer], from_right[layer]], axis=1)
            block = matmul(both, one_hot[rows : 3 * rows, lanes])
            at = slice(k * chans, (k + 1) * chans)
            picked[layer, at, :] = picked[layer, at, :] + block.astype(BF16)
        pre = matmul(enc_flat[layer], picked[layer])
        sig = jax.nn.sigmoid(pre)
        after = retained * (hidden.astype(F32) + pre * sig)
        own[layer + 1] = after.astype(BF16)

        @pl.when(layer < depth - 1)
        def _():
            start(halo(layer + 1))

        slope[layer] = sig * (1.0 + pre * (1.0 - sig))

    top_copies = across(own.at[depth], top_got, 2)
    for copy in top_copies:
        copy.start()
    joined = matmul(join[...], own[depth], ((0,), (0,)))
    for copy in join_copies:
        copy.wait_recv()
    unit_copies = across(unit_send, unit_got, 1)
    unit = unit_own[...]
    for i, copy in enumerate(unit_copies):
        copy.wait_recv()
        unit = unit + unit_got[i].astype(F32)
    for i, copy in enumerate(top_copies):
        copy.wait_recv()
        joined = joined + matmul(join_got[i], top_got[i], ((0,), (0,)))
    sig = jax.nn.sigmoid(joined)
    unit_slope = (sig * (1.0 + joined * (1.0 - sig))).astype(BF16).astype(F32)
    unit_grad = (unit * unit_slope).astype(BF16)
    grad[...] = matmul(join[...], unit_grad)

    @pl.loop(0, depth)
    def backward(step):
        layer = depth - 1 - step
        masked = retained * grad[...]
        act = (masked * slope[layer]).astype(BF16)
        terms = matmul(enc_t[layer], act).astype(BF16)
        terms = jnp.concatenate(
            [terms[k * chans : (k + 1) * chans] for k in range(taps)], axis=1
        )
        edge = matmul(terms, one_hot_t[:, rows : 3 * rows]).astype(BF16)
        edge_left[layer] = edge[:, :rows]
        edge_right[layer] = edge[:, rows:]
        start(back(layer))
        inner = masked + matmul(terms, one_hot_t[:, 0:rows])
        weight = matmul(act, picked[layer], ((1,), (1,)))
        for i in range(near_group):
            part_own[layer, i] = weight[i * share : (i + 1) * share].astype(BF16)
        for copy in scatter_copies(layer):
            copy.start()

        @pl.when(step >= 1)
        def _():
            sum_near(layer + 1)

        @pl.when(step >= 2)
        def _():
            sum_far(layer + 2)

        @pl.when(step >= 3)
        def _():
            finish(layer + 3)

        wait_recv(back(layer))
        grad[...] = inner + back_left[layer].astype(F32) + back_right[layer].astype(F32)

    map_out[...] = grad[...].astype(BF16)
    sum_near(0)
    sum_far(1)
    finish(2)
    sum_far(0)
    finish(1)
    finish(0)

    @pl.loop(0, depth)
    def drain(layer):
        wait_send(halo(layer))
        wait_send(back(layer))
        for copy in scatter_copies(layer) + level_copies(layer) + gather_copies(layer):
            copy.wait_send()

    wait_send(rims())
    for copy in join_copies + unit_copies + top_copies:
        copy.wait_send()


def per_device(n_sky, n_branch, sky_maps, footprint, neighbours, enc_weight, join_weight, dec_weight, cotangent):
    chans, rows = sky_maps.shape[1:]
    depth, taps = enc_weight.shape[1:3]
    width = dec_weight.shape[2]
    others = max(n_branch - 1, 1)
    near_group = math.gcd(n_sky, 4)
    far_group = n_sky // near_group
    share = chans // near_group
    near, far = max(near_group - 1, 1), max(far_group - 1, 1)
    vmem = pltpu.VMEM
    dma = pltpu.SemaphoreType.DMA
    layers = (depth, chans, rows)
    scratch = [
        vmem(footprint.shape, jnp.int32),
        vmem(neighbours.shape, jnp.int32),
        vmem(enc_weight.shape[1:], BF16),
        vmem((chans, width), BF16),
        vmem(dec_weight.shape, BF16),
        vmem(cotangent.shape, BF16),
        vmem((depth + 1, chans, rows), BF16),
        vmem(layers, BF16),
        vmem(layers, BF16),
        vmem((depth, taps * chans, rows), BF16),
        vmem(layers, F32),
        vmem((3 * rows, taps * rows), BF16),
        vmem((taps * rows, 3 * rows), BF16),
        vmem((128, rows), jnp.int32),
        vmem((depth, chans, taps * chans), BF16),
        vmem((depth, taps * chans, chans), BF16),
        vmem((chans, rows), F32),
        vmem(layers, BF16),
        vmem(layers, BF16),
        vmem(layers, BF16),
        vmem(layers, BF16),
        vmem((width, 3 * rows), F32),
        vmem((width, rows), BF16),
        vmem((width, rows), BF16),
        vmem((width, rows), BF16),
        vmem((width, rows), BF16),
        vmem((width, rows), F32),
        vmem((width, rows), BF16),
        vmem((others, width, rows), BF16),
        vmem((others, chans, width), BF16),
        vmem((others, chans, rows), BF16),
        vmem((depth, near_group, share, taps * chans), BF16),
        vmem((depth, near, share, taps * chans), BF16),
        vmem((depth, far_group, share, taps * chans), BF16),
        vmem((depth, near_group, share, taps * chans), BF16),
        dma((depth, 2)), dma((depth, 2)), dma((depth, 2)), dma((depth, 2)),
        dma((2,)), dma((2,)), dma((3, others)), dma((3, others)),
        dma((depth, near)), dma((depth, near)), dma((depth, far)), dma((depth, far)),
        dma((depth, near)), dma((depth, near)), dma((7,)),
    ]
    whole = pl.BlockSpec(memory_space=pltpu.VMEM)
    map_grad, tap_grads = pl.pallas_call(
        functools.partial(kernel, n_sky, n_branch, near_group),
        out_shape=(
            jax.ShapeDtypeStruct((chans, rows), BF16),
            jax.ShapeDtypeStruct((depth, taps, chans, chans), BF16),
        ),
        in_specs=[pl.BlockSpec(memory_space=pltpu.HBM)] * 7,
        out_specs=(whole, whole),
        scratch_shapes=scratch,
        compiler_params=pltpu.CompilerParams(
            collective_id=0, has_side_effects=True, vmem_limit_bytes=60 * 1024 * 1024
        ),
        name="unet_backward",
    )(sky_maps[0], footprint, neighbours, enc_weight[0], join_weight.T, dec_weight, cotangent)
    normalizer = 1.0 / math.sqrt(rows * n_sky)
    summed = tap_grads.astype(F32) * normalizer
    return map_grad[None], summed[None]


def solution(mesh):
    in_specs = (
        P("branch", None, "sky"),
        P("branch", "sky"),
        P(None, "sky"),
        P("branch", None, None, None, None),
        P(None, "branch"),
        P(None, "branch", None),
        P("branch", "sky"),
    )
    out_specs = (P("branch", None, "sky"), P("branch", None, None, None, None))
    return jax.shard_map(
        functools.partial(per_device, mesh.shape["sky"], mesh.shape["branch"]),
        mesh=mesh, in_specs=in_specs, out_specs=out_specs, check_vma=False,
    )
```

```python
import functools
import math

import jax
import jax.numpy as jnp
from jax import lax
from jax.experimental import pallas as pl
from jax.experimental.pallas import tpu as pltpu
from jax.sharding import PartitionSpec as P

MESH = pl.DeviceIdType.MESH
F32 = jnp.float32
BF16 = jnp.bfloat16


def matmul(a, b, contract=((1,), (0,))):
    return lax.dot_general(a, b, (contract, ((), ())), preferred_element_type=F32)


def kernel(
    n_sky, n_branch, near_group,
    maps_in, foot_in, nb_in, enc_in, join_in, dec_in, cot_in,
    map_out, grad_out,
    foot, nb, enc, join, dec, cot,
    own, from_side, picked, slope, one_hot, one_hot_t, rel, turned, enc_flat, enc_t,
    grad, edge, back_side, staged, map_own,
    dec_acc, rim_left, rim_right, got_left, got_right, unit_own, unit_send, unit_got,
    join_got, top_got,
    part_own, part_got, mid, final,
    fwd_send, fwd_recv, bwd_send, bwd_recv, rim_send, rim_recv, br_send, br_recv,
    near_send, near_recv, far_send, far_recv, out_send, out_recv, local_sem, store_sem,
):
    depth, taps = enc.shape[0], enc.shape[1]
    chans, rows = maps_in.shape
    far_group = n_sky // near_group
    share = chans // near_group
    sky = lax.axis_index("sky")
    branch = lax.axis_index("branch")
    has_left, has_right = sky > 0, sky < n_sky - 1
    left, right = jnp.maximum(sky - 1, 0), jnp.minimum(sky + 1, n_sky - 1)
    peers = [(d, lax.rem(branch + d, n_branch)) for d in range(1, n_branch)]

    mine = lax.rem(sky, near_group)
    level = sky // near_group
    mates = [
        (d, sky - mine + lax.rem(mine + d, near_group)) for d in range(1, near_group)
    ]
    stack = [
        (d, lax.rem(level + d, far_group) * near_group + mine) for d in range(1, far_group)
    ]

    sources = (maps_in, foot_in, nb_in, join_in, enc_in, dec_in, cot_in)
    targets = (own.at[0], foot, nb, join, enc, dec, cot)
    loads = [
        pltpu.make_async_copy(src, dst, local_sem.at[i])
        for i, (src, dst) in enumerate(zip(sources, targets))
    ]
    for load in loads:
        load.start()

    barrier = pltpu.get_barrier_semaphore()

    @pl.when(has_left)
    def _():
        pl.semaphore_signal(barrier, inc=1, device_id={"sky": left}, device_id_type=MESH)

    @pl.when(has_right)
    def _():
        pl.semaphore_signal(barrier, inc=1, device_id={"sky": right}, device_id_type=MESH)

    for _, peer in peers:
        pl.semaphore_signal(barrier, inc=1, device_id={"branch": peer}, device_id_type=MESH)
    for _, peer in mates + stack:
        pl.semaphore_signal(barrier, inc=1, device_id={"sky": peer}, device_id_type=MESH)
    pl.semaphore_wait(
        barrier,
        has_left.astype(jnp.int32) + has_right.astype(jnp.int32)
        + (n_branch - 1 + near_group - 1 + far_group - 1),
    )

    def to_left(src, dst, send, recv):
        return pltpu.make_async_remote_copy(
            src_ref=src, dst_ref=dst, send_sem=send, recv_sem=recv,
            device_id={"sky": left}, device_id_type=MESH,
        )

    def to_right(src, dst, send, recv):
        return pltpu.make_async_remote_copy(
            src_ref=src, dst_ref=dst, send_sem=send, recv_sem=recv,
            device_id={"sky": right}, device_id_type=MESH,
        )

    def halo(layer):
        return (
            to_left(own.at[layer], from_side.at[1, layer], fwd_send.at[layer, 0], fwd_recv.at[layer, 0]),
            to_right(own.at[layer], from_side.at[0, layer], fwd_send.at[layer, 1], fwd_recv.at[layer, 1]),
        )

    def back(layer):
        return (
            to_left(edge.at[0, layer], back_side.at[1, layer], bwd_send.at[layer, 0], bwd_recv.at[layer, 0]),
            to_right(edge.at[1, layer], back_side.at[0, layer], bwd_send.at[layer, 1], bwd_recv.at[layer, 1]),
        )

    def rims():
        return (
            to_left(rim_left, got_right, rim_send.at[0], rim_recv.at[0]),
            to_right(rim_right, got_left, rim_send.at[1], rim_recv.at[1]),
        )

    def start(pair):
        @pl.when(has_left)
        def _():
            pair[0].start()

        @pl.when(has_right)
        def _():
            pair[1].start()

    def wait_recv(pair):
        @pl.when(has_right)
        def _():
            pair[0].wait_recv()

        @pl.when(has_left)
        def _():
            pair[1].wait_recv()

    def wait_recv_side(pair, side):
        @pl.when(jnp.logical_and(side == 1, has_right))
        def _():
            pair[0].wait_recv()

        @pl.when(jnp.logical_and(side == 0, has_left))
        def _():
            pair[1].wait_recv()

    def start_side(pair, side):
        @pl.when(jnp.logical_and(side == 0, has_left))
        def _():
            pair[0].start()

        @pl.when(jnp.logical_and(side == 1, has_right))
        def _():
            pair[1].start()

    close = 1 - lax.rem(sky, 2)
    distant = 1 - close

    def wait_send(pair):
        @pl.when(has_left)
        def _():
            pair[0].wait_send()

        @pl.when(has_right)
        def _():
            pair[1].wait_send()

    def across(src, dst, kind):
        return [
            pltpu.make_async_remote_copy(
                src_ref=src, dst_ref=dst.at[d - 1],
                send_sem=br_send.at[kind, d - 1], recv_sem=br_recv.at[kind, d - 1],
                device_id={"branch": peer}, device_id_type=MESH,
            )
            for d, peer in peers
        ]

    def over_sky(peer, src, dst, send, recv):
        return pltpu.make_async_remote_copy(
            src_ref=src, dst_ref=dst, send_sem=send, recv_sem=recv,
            device_id={"sky": peer}, device_id_type=MESH,
        )

    def scatter_copies(layer):
        return [
            over_sky(
                peer, part_own.at[layer, lax.rem(mine + d, near_group)], part_got.at[layer, d - 1],
                near_send.at[layer, d - 1], near_recv.at[layer, d - 1],
            )
            for d, peer in mates
        ]

    def level_copies(layer):
        return [
            over_sky(
                peer, mid.at[layer, level], mid.at[layer, level],
                far_send.at[layer, d - 1], far_recv.at[layer, d - 1],
            )
            for d, peer in stack
        ]

    def gather_copies(layer):
        return [
            over_sky(
                peer, final.at[layer, mine], final.at[layer, mine],
                out_send.at[layer, d - 1], out_recv.at[layer, d - 1],
            )
            for d, peer in mates
        ]

    def sum_near(layer):
        total = part_own[layer, mine].astype(F32)
        for i, copy in enumerate(scatter_copies(layer)):
            copy.wait_recv()
            total = total + part_got[layer, i].astype(F32)
        mid[layer, level] = total.astype(BF16)
        for copy in level_copies(layer):
            copy.start()

    def sum_far(layer):
        for copy in level_copies(layer):
            copy.wait_recv()
        total = mid[layer, 0].astype(F32)
        for z in range(1, far_group):
            total = total + mid[layer, z].astype(F32)
        final[layer, mine] = total.astype(BF16)
        for copy in gather_copies(layer):
            copy.start()

    def store(layer):
        return pltpu.make_async_copy(staged.at[layer], grad_out.at[layer], store_sem.at[layer])

    def finish(layer):
        for copy in gather_copies(layer):
            copy.wait_recv()
        whole = jnp.concatenate([final[layer, i] for i in range(near_group)], axis=0)
        for k in range(taps):
            staged[layer, k] = whole[:, k * chans : (k + 1) * chans]
        store(layer).start()

    loads[0].wait()
    start(halo(0))
    loads[3].wait()
    join_copies = across(join, join_got, 0)
    for copy in join_copies:
        copy.start()

    @pl.when(jnp.logical_not(has_left))
    def _():
        from_side[0] = jnp.zeros(from_side.shape[1:], BF16)
        back_side[0] = jnp.zeros(back_side.shape[1:], BF16)
        got_left[...] = jnp.zeros_like(got_left)

    @pl.when(jnp.logical_not(has_right))
    def _():
        from_side[1] = jnp.zeros(from_side.shape[1:], BF16)
        back_side[1] = jnp.zeros(back_side.shape[1:], BF16)
        got_right[...] = jnp.zeros_like(got_right)

    loads[1].wait()
    loads[2].wait()
    first = (sky - 1) * rows
    near = nb[...]
    offset = jnp.where(near >= 0, near - first, -1)
    part = jnp.where(
        offset < 0, -1,
        jnp.where(offset < rows, offset + rows, jnp.where(offset < 2 * rows, offset - rows, offset)),
    )
    rel[...] = jnp.full(rel.shape, -1, jnp.int32)
    rel[0:taps, :] = part
    col = jnp.transpose(rel[...])
    turned[...] = col
    for k in range(taps):
        lanes = slice(k * rows, (k + 1) * rows)
        line = rel[k : k + 1, :]
        for p in range(3):
            index = lax.broadcasted_iota(jnp.int32, (rows, rows), 0) + p * rows
            one_hot[p * rows : (p + 1) * rows, lanes] = jnp.where(line == index, 1.0, 0.0).astype(BF16)
    for load in loads[4:]:
        load.wait()
    retained = foot[...].astype(F32)
    dec_acc[...] = jnp.zeros_like(dec_acc)
    dec_steps = 3

    @pl.loop(0, depth)
    def forward(layer):
        hidden = own[layer]
        for k in range(taps):
            block = matmul(hidden, one_hot[0:rows, k * rows : (k + 1) * rows])
            picked[layer, k * chans : (k + 1) * chans, :] = block.astype(BF16)
        for k in range(taps):
            tap = enc[layer, k]
            enc_flat[layer, :, k * chans : (k + 1) * chans] = tap
            enc_t[layer, k * chans : (k + 1) * chans, :] = jnp.transpose(tap)

        def decode(step):
            each = taps // dec_steps
            parts = []
            for k in range(step * each, (step + 1) * each):
                line = turned[:, k : k + 1]
                for p in range(3):
                    index = lax.broadcasted_iota(jnp.int32, (rows, rows), 1) + p * rows
                    one_hot_t[p, k * rows : (k + 1) * rows, :] = jnp.where(
                        line == index, 1.0, 0.0
                    ).astype(BF16)
                parts.append(matmul(dec[k], cot[...], ((0,), (0,))).astype(BF16))
            terms = jnp.concatenate(parts, axis=1)
            span = slice(step * each * rows, (step + 1) * each * rows)
            for p in range(3):
                dec_acc[p] = dec_acc[p] + matmul(terms, one_hot_t[p, span, :])

        for step in range(dec_steps):
            pl.when(layer == step)(functools.partial(decode, step))

        @pl.when(layer == dec_steps)
        def _():
            rim_left[...] = dec_acc[1].astype(BF16)
            rim_right[...] = dec_acc[2].astype(BF16)
            start(rims())

        @pl.when(layer == dec_steps + 1)
        def _():
            wait_recv(rims())
            total = dec_acc[0] + got_left[...].astype(F32) + got_right[...].astype(F32)
            unit_own[...] = total
            unit_send[...] = total.astype(BF16)
            for copy in across(unit_send, unit_got, 1):
                copy.start()

        for side in (close, distant):
            wait_recv_side(halo(layer), side)
            arrived = from_side[side, layer]
            table = pl.ds(pl.multiple_of((1 + side) * rows, rows), rows)
            for k in range(taps):
                block = matmul(arrived, one_hot[table, k * rows : (k + 1) * rows])
                at = slice(k * chans, (k + 1) * chans)
                picked[layer, at, :] = picked[layer, at, :] + block.astype(BF16)
        pre = matmul(enc_flat[layer], picked[layer])
        sig = jax.nn.sigmoid(pre)
        after = retained * (hidden.astype(F32) + pre * sig)
        own[layer + 1] = after.astype(BF16)

        @pl.when(layer < depth - 1)
        def _():
            start(halo(layer + 1))

        slope[layer] = sig * (1.0 + pre * (1.0 - sig))

    top_copies = across(own.at[depth], top_got, 2)
    for copy in top_copies:
        copy.start()
    joined = matmul(join[...], own[depth], ((0,), (0,)))
    for copy in join_copies:
        copy.wait_recv()
    unit_copies = across(unit_send, unit_got, 1)
    unit = unit_own[...]
    for i, copy in enumerate(unit_copies):
        copy.wait_recv()
        unit = unit + unit_got[i].astype(F32)
    for i, copy in enumerate(top_copies):
        copy.wait_recv()
        joined = joined + matmul(join_got[i], top_got[i], ((0,), (0,)))
    sig = jax.nn.sigmoid(joined)
    unit_slope = (sig * (1.0 + joined * (1.0 - sig))).astype(BF16).astype(F32)
    unit_grad = (unit * unit_slope).astype(BF16)
    grad[...] = matmul(join[...], unit_grad)

    def weigh(layer, act):
        weight = matmul(act, picked[layer], ((1,), (1,)))
        for i in range(near_group):
            part_own[layer, i] = weight[i * share : (i + 1) * share].astype(BF16)
        for copy in scatter_copies(layer):
            copy.start()

    def spread(layer, act):
        terms = matmul(enc_t[layer], act).astype(BF16)
        terms = jnp.concatenate(
            [terms[k * chans : (k + 1) * chans] for k in range(taps)], axis=1
        )
        for side in (distant, close):
            edge[side, layer] = matmul(terms, one_hot_t[1 + side]).astype(BF16)
            start_side(back(layer), side)
        return matmul(terms, one_hot_t[0])

    def take_back(layer, inner):
        wait_recv(back(layer))
        return inner + back_side[0, layer].astype(F32) + back_side[1, layer].astype(F32)

    @pl.loop(0, depth - 1)
    def backward(step):
        layer = depth - 1 - step
        masked = retained * grad[...]
        act = (masked * slope[layer]).astype(BF16)
        inner = masked + spread(layer, act)
        weigh(layer, act)

        @pl.when(step >= 1)
        def _():
            sum_near(layer + 1)

        @pl.when(step >= 2)
        def _():
            sum_far(layer + 2)

        @pl.when(step >= 3)
        def _():
            finish(layer + 3)

        grad[...] = take_back(layer, inner)

    masked = retained * grad[...]
    act = (masked * slope[0]).astype(BF16)
    weigh(0, act)
    inner = masked + spread(0, act)
    late = [k for k in (1, 2, 3) if k < depth]
    for k, stage in zip(late, (sum_near, sum_far, finish)):
        stage(k)
    sum_near(0)
    if depth > 1:
        sum_far(1)
    if depth > 2:
        finish(2)
    map_own[...] = take_back(0, inner).astype(BF16)
    map_copy = pltpu.make_async_copy(map_own, map_out, local_sem.at[0])
    map_copy.start()
    sum_far(0)
    if depth > 1:
        finish(1)
    finish(0)
    map_copy.wait()

    @pl.loop(0, depth)
    def drain(layer):
        wait_send(halo(layer))
        wait_send(back(layer))
        store(layer).wait()
        for copy in scatter_copies(layer) + level_copies(layer) + gather_copies(layer):
            copy.wait_send()

    wait_send(rims())
    for copy in join_copies + unit_copies + top_copies:
        copy.wait_send()


def scale_kernel(normalizer, map_in, sums_in, map_out, sums_out, held, sums, scaled, in_sem, out_sem):
    depth = sums_in.shape[0]
    reads = [pltpu.make_async_copy(sums_in.at[i], sums.at[i], in_sem.at[i]) for i in range(depth)]
    writes = [
        pltpu.make_async_copy(scaled.at[i], sums_out.at[i], out_sem.at[i]) for i in range(depth)
    ]
    reads.append(pltpu.make_async_copy(map_in, held, in_sem.at[depth]))
    writes.append(pltpu.make_async_copy(held, map_out, out_sem.at[depth]))
    for read in reads:
        read.start()
    for i in range(depth):
        reads[i].wait()
        scaled[i] = sums[i].astype(F32) * normalizer
        writes[i].start()
    reads[depth].wait()
    writes[depth].start()
    for write in writes:
        write.wait()


def per_device(n_sky, n_branch, sky_maps, footprint, neighbours, enc_weight, join_weight, dec_weight, cotangent):
    chans, rows = sky_maps.shape[1:]
    depth, taps = enc_weight.shape[1:3]
    width = dec_weight.shape[2]
    others = max(n_branch - 1, 1)
    near_group = math.gcd(n_sky, 4)
    far_group = n_sky // near_group
    share = chans // near_group
    near, far = max(near_group - 1, 1), max(far_group - 1, 1)
    vmem = pltpu.VMEM
    dma = pltpu.SemaphoreType.DMA
    layers = (depth, chans, rows)
    scratch = [
        vmem(footprint.shape, jnp.int32),
        vmem(neighbours.shape, jnp.int32),
        vmem(enc_weight.shape[1:], BF16),
        vmem((chans, width), BF16),
        vmem(dec_weight.shape, BF16),
        vmem(cotangent.shape, BF16),
        vmem((depth + 1, chans, rows), BF16),
        vmem((2,) + layers, BF16),
        vmem((depth, taps * chans, rows), BF16),
        vmem(layers, F32),
        vmem((3 * rows, taps * rows), BF16),
        vmem((3, taps * rows, rows), BF16),
        vmem((128, rows), jnp.int32),
        vmem((rows, 128), jnp.int32),
        vmem((depth, chans, taps * chans), BF16),
        vmem((depth, taps * chans, chans), BF16),
        vmem((chans, rows), F32),
        vmem((2,) + layers, BF16),
        vmem((2,) + layers, BF16),
        vmem((depth, taps, chans, chans), BF16),
        vmem((chans, rows), BF16),
        vmem((3, width, rows), F32),
        vmem((width, rows), BF16),
        vmem((width, rows), BF16),
        vmem((width, rows), BF16),
        vmem((width, rows), BF16),
        vmem((width, rows), F32),
        vmem((width, rows), BF16),
        vmem((others, width, rows), BF16),
        vmem((others, chans, width), BF16),
        vmem((others, chans, rows), BF16),
        vmem((depth, near_group, share, taps * chans), BF16),
        vmem((depth, near, share, taps * chans), BF16),
        vmem((depth, far_group, share, taps * chans), BF16),
        vmem((depth, near_group, share, taps * chans), BF16),
        dma((depth, 2)), dma((depth, 2)), dma((depth, 2)), dma((depth, 2)),
        dma((2,)), dma((2,)), dma((3, others)), dma((3, others)),
        dma((depth, near)), dma((depth, near)), dma((depth, far)), dma((depth, far)),
        dma((depth, near)), dma((depth, near)), dma((7,)), dma((depth,)),
    ]
    hbm = pl.BlockSpec(memory_space=pltpu.HBM)
    map_grad, tap_grads = pl.pallas_call(
        functools.partial(kernel, n_sky, n_branch, near_group),
        out_shape=(
            jax.ShapeDtypeStruct((chans, rows), BF16),
            jax.ShapeDtypeStruct((depth, taps, chans, chans), BF16),
        ),
        in_specs=[hbm] * 7,
        out_specs=(hbm, hbm),
        scratch_shapes=scratch,
        compiler_params=pltpu.CompilerParams(
            collective_id=0, has_side_effects=True, vmem_limit_bytes=60 * 1024 * 1024
        ),
        name="unet_backward",
    )(sky_maps[0], footprint, neighbours, enc_weight[0], join_weight.T, dec_weight, cotangent)
    normalizer = 1.0 / math.sqrt(rows * n_sky)
    map_grad, summed = pl.pallas_call(
        functools.partial(scale_kernel, normalizer),
        out_shape=(
            jax.ShapeDtypeStruct((chans, rows), BF16),
            jax.ShapeDtypeStruct((depth, taps, chans, chans), F32),
        ),
        in_specs=[hbm] * 2,
        out_specs=(hbm, hbm),
        scratch_shapes=[
            vmem((chans, rows), BF16),
            vmem((depth, taps, chans, chans), BF16),
            vmem((depth, taps, chans, chans), F32),
            dma((depth + 1,)),
            dma((depth + 1,)),
        ],
        compiler_params=pltpu.CompilerParams(vmem_limit_bytes=60 * 1024 * 1024),
        name="scale_sums",
    )(map_grad, tap_grads)
    return map_grad[None], summed[None]


def solution(mesh):
    in_specs = (
        P("branch", None, "sky"),
        P("branch", "sky"),
        P(None, "sky"),
        P("branch", None, None, None, None),
        P(None, "branch"),
        P(None, "branch", None),
        P("branch", "sky"),
    )
    out_specs = (P("branch", None, "sky"), P("branch", None, None, None, None))
    return jax.shard_map(
        functools.partial(per_device, mesh.shape["sky"], mesh.shape["branch"]),
        mesh=mesh, in_specs=in_specs, out_specs=out_specs, check_vma=False,
    )
```

```python
import functools
import math

import jax
import jax.numpy as jnp
from jax import lax
from jax.experimental import pallas as pl
from jax.experimental.pallas import tpu as pltpu
from jax.sharding import PartitionSpec as P

MESH = pl.DeviceIdType.MESH
F32 = jnp.float32
BF16 = jnp.bfloat16


def matmul(a, b, contract=((1,), (0,))):
    return lax.dot_general(a, b, (contract, ((), ())), preferred_element_type=F32)


def kernel(
    n_sky, n_branch, near_group,
    maps_in, foot_in, nb_in, enc_in, join_in, dec_in, cot_in,
    map_out, grad_out,
    foot, nb, enc, join, dec, cot,
    own, from_side, picked, slope, one_hot, one_hot_t, rel, turned, enc_flat, enc_t,
    grad, edge, back_side, staged, map_own,
    dec_acc, rim_left, rim_right, got_left, got_right, unit_own, unit_send, unit_got,
    join_got, top_got,
    part_own, part_got, mid, final,
    fwd_send, fwd_recv, bwd_send, bwd_recv, rim_send, rim_recv, br_send, br_recv,
    near_send, near_recv, far_send, far_recv, out_send, out_recv, local_sem, store_sem,
):
    depth, taps = enc.shape[0], enc.shape[1]
    chans, rows = maps_in.shape
    far_group = n_sky // near_group
    share = chans // near_group
    sky = lax.axis_index("sky")
    branch = lax.axis_index("branch")
    has_left, has_right = sky > 0, sky < n_sky - 1
    left, right = jnp.maximum(sky - 1, 0), jnp.minimum(sky + 1, n_sky - 1)
    peers = [(d, lax.rem(branch + d, n_branch)) for d in range(1, n_branch)]

    mine = lax.rem(sky, near_group)
    level = sky // near_group
    mates = [
        (d, sky - mine + lax.rem(mine + d, near_group)) for d in range(1, near_group)
    ]
    stack = [
        (d, lax.rem(level + d, far_group) * near_group + mine) for d in range(1, far_group)
    ]

    sources = (maps_in, foot_in, nb_in, join_in, enc_in, dec_in, cot_in)
    targets = (own.at[0], foot, nb, join, enc, dec, cot)
    loads = [
        pltpu.make_async_copy(src, dst, local_sem.at[i])
        for i, (src, dst) in enumerate(zip(sources, targets))
    ]
    for load in loads:
        load.start()

    barrier = pltpu.get_barrier_semaphore()

    @pl.when(has_left)
    def _():
        pl.semaphore_signal(barrier, inc=1, device_id={"sky": left}, device_id_type=MESH)

    @pl.when(has_right)
    def _():
        pl.semaphore_signal(barrier, inc=1, device_id={"sky": right}, device_id_type=MESH)

    for _, peer in peers:
        pl.semaphore_signal(barrier, inc=1, device_id={"branch": peer}, device_id_type=MESH)
    for _, peer in mates + stack:
        pl.semaphore_signal(barrier, inc=1, device_id={"sky": peer}, device_id_type=MESH)
    pl.semaphore_wait(
        barrier,
        has_left.astype(jnp.int32) + has_right.astype(jnp.int32)
        + (n_branch - 1 + near_group - 1 + far_group - 1),
    )

    def to_left(src, dst, send, recv):
        return pltpu.make_async_remote_copy(
            src_ref=src, dst_ref=dst, send_sem=send, recv_sem=recv,
            device_id={"sky": left}, device_id_type=MESH,
        )

    def to_right(src, dst, send, recv):
        return pltpu.make_async_remote_copy(
            src_ref=src, dst_ref=dst, send_sem=send, recv_sem=recv,
            device_id={"sky": right}, device_id_type=MESH,
        )

    def halo(layer):
        return (
            to_left(own.at[layer], from_side.at[1, layer], fwd_send.at[layer, 0], fwd_recv.at[layer, 0]),
            to_right(own.at[layer], from_side.at[0, layer], fwd_send.at[layer, 1], fwd_recv.at[layer, 1]),
        )

    def back(layer):
        return (
            to_left(edge.at[0, layer], back_side.at[1, layer], bwd_send.at[layer, 0], bwd_recv.at[layer, 0]),
            to_right(edge.at[1, layer], back_side.at[0, layer], bwd_send.at[layer, 1], bwd_recv.at[layer, 1]),
        )

    def rims():
        return (
            to_left(rim_left, got_right, rim_send.at[0], rim_recv.at[0]),
            to_right(rim_right, got_left, rim_send.at[1], rim_recv.at[1]),
        )

    def start(pair):
        @pl.when(has_left)
        def _():
            pair[0].start()

        @pl.when(has_right)
        def _():
            pair[1].start()

    def wait_recv(pair):
        @pl.when(has_right)
        def _():
            pair[0].wait_recv()

        @pl.when(has_left)
        def _():
            pair[1].wait_recv()

    def wait_recv_side(pair, side):
        @pl.when(jnp.logical_and(side == 1, has_right))
        def _():
            pair[0].wait_recv()

        @pl.when(jnp.logical_and(side == 0, has_left))
        def _():
            pair[1].wait_recv()

    def start_side(pair, side):
        @pl.when(jnp.logical_and(side == 0, has_left))
        def _():
            pair[0].start()

        @pl.when(jnp.logical_and(side == 1, has_right))
        def _():
            pair[1].start()

    close = 1 - lax.rem(sky, 2)
    distant = 1 - close

    def wait_send(pair):
        @pl.when(has_left)
        def _():
            pair[0].wait_send()

        @pl.when(has_right)
        def _():
            pair[1].wait_send()

    def across(src, dst, kind):
        return [
            pltpu.make_async_remote_copy(
                src_ref=src, dst_ref=dst.at[d - 1],
                send_sem=br_send.at[kind, d - 1], recv_sem=br_recv.at[kind, d - 1],
                device_id={"branch": peer}, device_id_type=MESH,
            )
            for d, peer in peers
        ]

    def over_sky(peer, src, dst, send, recv):
        return pltpu.make_async_remote_copy(
            src_ref=src, dst_ref=dst, send_sem=send, recv_sem=recv,
            device_id={"sky": peer}, device_id_type=MESH,
        )

    def scatter_copies(layer):
        return [
            over_sky(
                peer, part_own.at[layer, lax.rem(mine + d, near_group)], part_got.at[layer, d - 1],
                near_send.at[layer, d - 1], near_recv.at[layer, d - 1],
            )
            for d, peer in mates
        ]

    def level_copies(layer):
        return [
            over_sky(
                peer, mid.at[layer, level], mid.at[layer, level],
                far_send.at[layer, d - 1], far_recv.at[layer, d - 1],
            )
            for d, peer in stack
        ]

    def gather_copies(layer):
        return [
            over_sky(
                peer, final.at[layer, mine], final.at[layer, mine],
                out_send.at[layer, d - 1], out_recv.at[layer, d - 1],
            )
            for d, peer in mates
        ]

    def sum_near(layer):
        total = part_own[layer, mine].astype(F32)
        for i, copy in enumerate(scatter_copies(layer)):
            copy.wait_recv()
            total = total + part_got[layer, i].astype(F32)
        mid[layer, level] = total.astype(BF16)
        for copy in level_copies(layer):
            copy.start()

    def sum_far(layer):
        for copy in level_copies(layer):
            copy.wait_recv()
        total = mid[layer, 0].astype(F32)
        for z in range(1, far_group):
            total = total + mid[layer, z].astype(F32)
        final[layer, mine] = total.astype(BF16)
        for copy in gather_copies(layer):
            copy.start()

    def store(layer):
        return pltpu.make_async_copy(staged.at[layer], grad_out.at[layer], store_sem.at[layer])

    def finish(layer):
        for copy in gather_copies(layer):
            copy.wait_recv()
        whole = jnp.concatenate([final[layer, i] for i in range(near_group)], axis=0)
        for k in range(taps):
            staged[layer, k] = whole[:, k * chans : (k + 1) * chans]
        store(layer).start()

    loads[0].wait()
    start(halo(0))
    loads[3].wait()
    join_copies = across(join, join_got, 0)
    for copy in join_copies:
        copy.start()

    @pl.when(jnp.logical_not(has_left))
    def _():
        from_side[0] = jnp.zeros(from_side.shape[1:], BF16)
        back_side[0] = jnp.zeros(back_side.shape[1:], BF16)
        got_left[...] = jnp.zeros_like(got_left)

    @pl.when(jnp.logical_not(has_right))
    def _():
        from_side[1] = jnp.zeros(from_side.shape[1:], BF16)
        back_side[1] = jnp.zeros(back_side.shape[1:], BF16)
        got_right[...] = jnp.zeros_like(got_right)

    loads[1].wait()
    loads[2].wait()
    first = (sky - 1) * rows
    near = nb[...]
    offset = jnp.where(near >= 0, near - first, -1)
    part = jnp.where(
        offset < 0, -1,
        jnp.where(offset < rows, offset + rows, jnp.where(offset < 2 * rows, offset - rows, offset)),
    )
    rel[...] = jnp.full(rel.shape, -1, jnp.int32)
    rel[0:taps, :] = part
    col = jnp.transpose(rel[...])
    turned[...] = col
    for k in range(taps):
        lanes = slice(k * rows, (k + 1) * rows)
        line = rel[k : k + 1, :]
        for p in range(3):
            index = lax.broadcasted_iota(jnp.int32, (rows, rows), 0) + p * rows
            one_hot[p * rows : (p + 1) * rows, lanes] = jnp.where(line == index, 1.0, 0.0).astype(BF16)
    for load in loads[4:]:
        load.wait()
    retained = foot[...].astype(F32)
    dec_acc[...] = jnp.zeros_like(dec_acc)
    dec_cuts = [0, taps // 9, 4 * taps // 9, 7 * taps // 9, taps]
    dec_steps = len(dec_cuts) - 1

    @pl.loop(0, depth)
    def forward(layer):
        hidden = own[layer]
        for k in range(taps):
            block = matmul(hidden, one_hot[0:rows, k * rows : (k + 1) * rows])
            picked[layer, k * chans : (k + 1) * chans, :] = block.astype(BF16)
        for k in range(taps):
            tap = enc[layer, k]
            enc_flat[layer, :, k * chans : (k + 1) * chans] = tap
            enc_t[layer, :, k * chans : (k + 1) * chans] = jnp.transpose(tap)

        def decode(step):
            low, high = dec_cuts[step], dec_cuts[step + 1]
            parts = []
            for k in range(low, high):
                line = turned[:, k : k + 1]
                for p in range(3):
                    index = lax.broadcasted_iota(jnp.int32, (rows, rows), 1) + p * rows
                    one_hot_t[p, k * rows : (k + 1) * rows, :] = jnp.where(
                        line == index, 1.0, 0.0
                    ).astype(BF16)
                parts.append(matmul(dec[k], cot[...], ((0,), (0,))).astype(BF16))
            terms = jnp.concatenate(parts, axis=1)
            span = slice(low * rows, high * rows)
            for p in range(3):
                dec_acc[p] = dec_acc[p] + matmul(terms, one_hot_t[p, span, :])

        for step in range(dec_steps):
            pl.when(layer == step)(functools.partial(decode, step))

        @pl.when(layer == dec_steps)
        def _():
            rim_left[...] = dec_acc[1].astype(BF16)
            rim_right[...] = dec_acc[2].astype(BF16)
            start(rims())

        @pl.when(layer == dec_steps + 1)
        def _():
            wait_recv(rims())
            total = dec_acc[0] + got_left[...].astype(F32) + got_right[...].astype(F32)
            unit_own[...] = total
            unit_send[...] = total.astype(BF16)
            for copy in across(unit_send, unit_got, 1):
                copy.start()

        for side in (close, distant):
            wait_recv_side(halo(layer), side)
            arrived = from_side[side, layer]
            table = pl.ds(pl.multiple_of((1 + side) * rows, rows), rows)
            for k in range(taps):
                block = matmul(arrived, one_hot[table, k * rows : (k + 1) * rows])
                at = slice(k * chans, (k + 1) * chans)
                picked[layer, at, :] = picked[layer, at, :] + block.astype(BF16)
        pre = matmul(enc_flat[layer], picked[layer])
        sig = jax.nn.sigmoid(pre)
        after = retained * (hidden.astype(F32) + pre * sig)
        own[layer + 1] = after.astype(BF16)

        @pl.when(layer < depth - 1)
        def _():
            start(halo(layer + 1))

        slope[layer] = sig * (1.0 + pre * (1.0 - sig))

    top_copies = across(own.at[depth], top_got, 2)
    for copy in top_copies:
        copy.start()
    joined = matmul(join[...], own[depth], ((0,), (0,)))
    for copy in join_copies:
        copy.wait_recv()
    unit_copies = across(unit_send, unit_got, 1)
    unit = unit_own[...]
    for i, copy in enumerate(unit_copies):
        copy.wait_recv()
        unit = unit + unit_got[i].astype(F32)
    for i, copy in enumerate(top_copies):
        copy.wait_recv()
        joined = joined + matmul(join_got[i], top_got[i], ((0,), (0,)))
    sig = jax.nn.sigmoid(joined)
    unit_slope = (sig * (1.0 + joined * (1.0 - sig))).astype(BF16).astype(F32)
    unit_grad = (unit * unit_slope).astype(BF16)
    grad[...] = matmul(join[...], unit_grad)

    def weigh(layer, act):
        weight = matmul(act, picked[layer], ((1,), (1,)))
        for i in range(near_group):
            part_own[layer, i] = weight[i * share : (i + 1) * share].astype(BF16)
        for copy in scatter_copies(layer):
            copy.start()

    def spread(layer, act):
        def placed(part):
            spots = [
                matmul(act, one_hot_t[part, k * rows : (k + 1) * rows, :]).astype(BF16)
                for k in range(taps)
            ]
            return matmul(enc_t[layer], jnp.concatenate(spots, axis=0))

        for side in (distant, close):
            edge[side, layer] = placed(1 + side).astype(BF16)
            start_side(back(layer), side)
        return placed(0)

    def take_back(layer, inner):
        wait_recv(back(layer))
        return inner + back_side[0, layer].astype(F32) + back_side[1, layer].astype(F32)

    @pl.loop(0, depth - 1)
    def backward(step):
        layer = depth - 1 - step
        masked = retained * grad[...]
        act = (masked * slope[layer]).astype(BF16)
        inner = masked + spread(layer, act)
        weigh(layer, act)

        @pl.when(step >= 1)
        def _():
            sum_near(layer + 1)

        @pl.when(step >= 3)
        def _():
            sum_far(layer + 3)

        grad[...] = take_back(layer, inner)

    masked = retained * grad[...]
    act = (masked * slope[0]).astype(BF16)
    weigh(0, act)
    inner = masked + spread(0, act)
    if depth > 1:
        sum_near(1)
    for k in (3, 2):
        if k < depth:
            sum_far(k)
    sum_near(0)
    for k in (5, 4):
        if k < depth:
            finish(k)
    if depth > 1:
        sum_far(1)
    map_own[...] = take_back(0, inner).astype(BF16)
    map_copy = pltpu.make_async_copy(map_own, map_out, local_sem.at[0])
    map_copy.start()
    for k in (3, 2):
        if k < depth:
            finish(k)
    sum_far(0)
    if depth > 1:
        finish(1)
    finish(0)
    map_copy.wait()

    @pl.loop(0, depth)
    def drain(layer):
        wait_send(halo(layer))
        wait_send(back(layer))
        store(layer).wait()
        for copy in scatter_copies(layer) + level_copies(layer) + gather_copies(layer):
            copy.wait_send()

    wait_send(rims())
    for copy in join_copies + unit_copies + top_copies:
        copy.wait_send()


def scale_kernel(normalizer, map_in, sums_in, map_out, sums_out, held, sums, scaled, in_sem, out_sem):
    depth = sums_in.shape[0]
    reads = [pltpu.make_async_copy(sums_in.at[i], sums.at[i], in_sem.at[i]) for i in range(depth)]
    writes = [
        pltpu.make_async_copy(scaled.at[i], sums_out.at[i], out_sem.at[i]) for i in range(depth)
    ]
    reads.append(pltpu.make_async_copy(map_in, held, in_sem.at[depth]))
    writes.append(pltpu.make_async_copy(held, map_out, out_sem.at[depth]))
    for read in reads:
        read.start()
    for i in range(depth):
        reads[i].wait()
        scaled[i] = sums[i].astype(F32) * normalizer
        writes[i].start()
    reads[depth].wait()
    writes[depth].start()
    for write in writes:
        write.wait()


def per_device(n_sky, n_branch, sky_maps, footprint, neighbours, enc_weight, join_weight, dec_weight, cotangent):
    chans, rows = sky_maps.shape[1:]
    depth, taps = enc_weight.shape[1:3]
    width = dec_weight.shape[2]
    others = max(n_branch - 1, 1)
    near_group = math.gcd(n_sky, 4)
    far_group = n_sky // near_group
    share = chans // near_group
    near, far = max(near_group - 1, 1), max(far_group - 1, 1)
    vmem = pltpu.VMEM
    dma = pltpu.SemaphoreType.DMA
    layers = (depth, chans, rows)
    scratch = [
        vmem(footprint.shape, jnp.int32),
        vmem(neighbours.shape, jnp.int32),
        vmem(enc_weight.shape[1:], BF16),
        vmem((chans, width), BF16),
        vmem(dec_weight.shape, BF16),
        vmem(cotangent.shape, BF16),
        vmem((depth + 1, chans, rows), BF16),
        vmem((2,) + layers, BF16),
        vmem((depth, taps * chans, rows), BF16),
        vmem(layers, F32),
        vmem((3 * rows, taps * rows), BF16),
        vmem((3, taps * rows, rows), BF16),
        vmem((128, rows), jnp.int32),
        vmem((rows, 128), jnp.int32),
        vmem((depth, chans, taps * chans), BF16),
        vmem((depth, chans, taps * chans), BF16),
        vmem((chans, rows), F32),
        vmem((2,) + layers, BF16),
        vmem((2,) + layers, BF16),
        vmem((depth, taps, chans, chans), BF16),
        vmem((chans, rows), BF16),
        vmem((3, width, rows), F32),
        vmem((width, rows), BF16),
        vmem((width, rows), BF16),
        vmem((width, rows), BF16),
        vmem((width, rows), BF16),
        vmem((width, rows), F32),
        vmem((width, rows), BF16),
        vmem((others, width, rows), BF16),
        vmem((others, chans, width), BF16),
        vmem((others, chans, rows), BF16),
        vmem((depth, near_group, share, taps * chans), BF16),
        vmem((depth, near, share, taps * chans), BF16),
        vmem((depth, far_group, share, taps * chans), BF16),
        vmem((depth, near_group, share, taps * chans), BF16),
        dma((depth, 2)), dma((depth, 2)), dma((depth, 2)), dma((depth, 2)),
        dma((2,)), dma((2,)), dma((3, others)), dma((3, others)),
        dma((depth, near)), dma((depth, near)), dma((depth, far)), dma((depth, far)),
        dma((depth, near)), dma((depth, near)), dma((7,)), dma((depth,)),
    ]
    hbm = pl.BlockSpec(memory_space=pltpu.HBM)
    map_grad, tap_grads = pl.pallas_call(
        functools.partial(kernel, n_sky, n_branch, near_group),
        out_shape=(
            jax.ShapeDtypeStruct((chans, rows), BF16),
            jax.ShapeDtypeStruct((depth, taps, chans, chans), BF16),
        ),
        in_specs=[hbm] * 7,
        out_specs=(hbm, hbm),
        scratch_shapes=scratch,
        compiler_params=pltpu.CompilerParams(
            collective_id=0, has_side_effects=True, vmem_limit_bytes=60 * 1024 * 1024
        ),
        name="unet_backward",
    )(sky_maps[0], footprint, neighbours, enc_weight[0], join_weight.T, dec_weight, cotangent)
    normalizer = 1.0 / math.sqrt(rows * n_sky)
    map_grad, summed = pl.pallas_call(
        functools.partial(scale_kernel, normalizer),
        out_shape=(
            jax.ShapeDtypeStruct((chans, rows), BF16),
            jax.ShapeDtypeStruct((depth, taps, chans, chans), F32),
        ),
        in_specs=[hbm] * 2,
        out_specs=(hbm, hbm),
        scratch_shapes=[
            vmem((chans, rows), BF16),
            vmem((depth, taps, chans, chans), BF16),
            vmem((depth, taps, chans, chans), F32),
            dma((depth + 1,)),
            dma((depth + 1,)),
        ],
        compiler_params=pltpu.CompilerParams(vmem_limit_bytes=60 * 1024 * 1024),
        name="scale_sums",
    )(map_grad, tap_grads)
    return map_grad[None], summed[None]


def solution(mesh):
    in_specs = (
        P("branch", None, "sky"),
        P("branch", "sky"),
        P(None, "sky"),
        P("branch", None, None, None, None),
        P(None, "branch"),
        P(None, "branch", None),
        P("branch", "sky"),
    )
    out_specs = (P("branch", None, "sky"), P("branch", None, None, None, None))
    return jax.shard_map(
        functools.partial(per_device, mesh.shape["sky"], mesh.shape["branch"]),
        mesh=mesh, in_specs=in_specs, out_specs=out_specs, check_vma=False,
    )
```

```python
import functools
import math

import jax
import jax.numpy as jnp
from jax import lax
from jax.experimental import pallas as pl
from jax.experimental.pallas import tpu as pltpu
from jax.sharding import PartitionSpec as P

MESH = pl.DeviceIdType.MESH
F32 = jnp.float32
BF16 = jnp.bfloat16


def matmul(a, b, contract=((1,), (0,))):
    return lax.dot_general(a, b, (contract, ((), ())), preferred_element_type=F32)


def kernel(
    n_sky, n_branch, near_group,
    maps_in, foot_in, nb_in, enc_in, join_in, dec_in, cot_in,
    map_out, grad_out,
    foot, nb, enc, join, dec, cot,
    own, from_side, picked, slope, one_hot, one_hot_t, rel, turned, enc_flat, enc_t,
    grad, edge, back_side, staged, map_own,
    dec_acc, rim_left, rim_right, got_left, got_right, unit_own, unit_send, unit_got,
    join_got, top_got,
    part_own, part_got, mid, final,
    fwd_send, fwd_recv, bwd_send, bwd_recv, rim_send, rim_recv, br_send, br_recv,
    near_send, near_recv, far_send, far_recv, out_send, out_recv, local_sem, store_sem,
):
    depth, taps = enc.shape[0], enc.shape[1]
    chans, rows = maps_in.shape
    far_group = n_sky // near_group
    share = chans // near_group
    sky = lax.axis_index("sky")
    branch = lax.axis_index("branch")
    has_left, has_right = sky > 0, sky < n_sky - 1
    left, right = jnp.maximum(sky - 1, 0), jnp.minimum(sky + 1, n_sky - 1)
    peers = [(d, lax.rem(branch + d, n_branch)) for d in range(1, n_branch)]

    mine = lax.rem(sky, near_group)
    level = sky // near_group
    mates = [
        (d, sky - mine + lax.rem(mine + d, near_group)) for d in range(1, near_group)
    ]
    stack = [
        (d, lax.rem(level + d, far_group) * near_group + mine) for d in range(1, far_group)
    ]

    sources = (maps_in, foot_in, nb_in, join_in, enc_in, dec_in, cot_in)
    targets = (own.at[0], foot, nb, join, enc, dec, cot)
    loads = [
        pltpu.make_async_copy(src, dst, local_sem.at[i])
        for i, (src, dst) in enumerate(zip(sources, targets))
    ]
    for load in loads:
        load.start()

    barrier = pltpu.get_barrier_semaphore()

    @pl.when(has_left)
    def _():
        pl.semaphore_signal(barrier, inc=1, device_id={"sky": left}, device_id_type=MESH)

    @pl.when(has_right)
    def _():
        pl.semaphore_signal(barrier, inc=1, device_id={"sky": right}, device_id_type=MESH)

    for _, peer in peers:
        pl.semaphore_signal(barrier, inc=1, device_id={"branch": peer}, device_id_type=MESH)
    for _, peer in mates + stack:
        pl.semaphore_signal(barrier, inc=1, device_id={"sky": peer}, device_id_type=MESH)
    def to_left(src, dst, send, recv):
        return pltpu.make_async_remote_copy(
            src_ref=src, dst_ref=dst, send_sem=send, recv_sem=recv,
            device_id={"sky": left}, device_id_type=MESH,
        )

    def to_right(src, dst, send, recv):
        return pltpu.make_async_remote_copy(
            src_ref=src, dst_ref=dst, send_sem=send, recv_sem=recv,
            device_id={"sky": right}, device_id_type=MESH,
        )

    def halo(layer):
        return (
            to_left(own.at[layer], from_side.at[1, layer], fwd_send.at[layer, 0], fwd_recv.at[layer, 0]),
            to_right(own.at[layer], from_side.at[0, layer], fwd_send.at[layer, 1], fwd_recv.at[layer, 1]),
        )

    def back(layer):
        return (
            to_left(edge.at[0, layer], back_side.at[1, layer], bwd_send.at[layer, 0], bwd_recv.at[layer, 0]),
            to_right(edge.at[1, layer], back_side.at[0, layer], bwd_send.at[layer, 1], bwd_recv.at[layer, 1]),
        )

    def rims():
        return (
            to_left(rim_left, got_right, rim_send.at[0], rim_recv.at[0]),
            to_right(rim_right, got_left, rim_send.at[1], rim_recv.at[1]),
        )

    def start(pair):
        @pl.when(has_left)
        def _():
            pair[0].start()

        @pl.when(has_right)
        def _():
            pair[1].start()

    def wait_recv(pair):
        @pl.when(has_right)
        def _():
            pair[0].wait_recv()

        @pl.when(has_left)
        def _():
            pair[1].wait_recv()

    def wait_recv_side(pair, side):
        @pl.when(jnp.logical_and(side == 1, has_right))
        def _():
            pair[0].wait_recv()

        @pl.when(jnp.logical_and(side == 0, has_left))
        def _():
            pair[1].wait_recv()

    def start_side(pair, side):
        @pl.when(jnp.logical_and(side == 0, has_left))
        def _():
            pair[0].start()

        @pl.when(jnp.logical_and(side == 1, has_right))
        def _():
            pair[1].start()

    close = 1 - lax.rem(sky, 2)
    distant = 1 - close

    def wait_send(pair):
        @pl.when(has_left)
        def _():
            pair[0].wait_send()

        @pl.when(has_right)
        def _():
            pair[1].wait_send()

    def across(src, dst, kind):
        return [
            pltpu.make_async_remote_copy(
                src_ref=src, dst_ref=dst.at[d - 1],
                send_sem=br_send.at[kind, d - 1], recv_sem=br_recv.at[kind, d - 1],
                device_id={"branch": peer}, device_id_type=MESH,
            )
            for d, peer in peers
        ]

    def over_sky(peer, src, dst, send, recv):
        return pltpu.make_async_remote_copy(
            src_ref=src, dst_ref=dst, send_sem=send, recv_sem=recv,
            device_id={"sky": peer}, device_id_type=MESH,
        )

    def scatter_copies(layer):
        return [
            over_sky(
                peer, part_own.at[layer, lax.rem(mine + d, near_group)], part_got.at[layer, d - 1],
                near_send.at[layer, d - 1], near_recv.at[layer, d - 1],
            )
            for d, peer in mates
        ]

    def level_copies(layer):
        return [
            over_sky(
                peer, mid.at[layer, level], mid.at[layer, level],
                far_send.at[layer, d - 1], far_recv.at[layer, d - 1],
            )
            for d, peer in stack
        ]

    def gather_copies(layer):
        return [
            over_sky(
                peer, final.at[layer, mine], final.at[layer, mine],
                out_send.at[layer, d - 1], out_recv.at[layer, d - 1],
            )
            for d, peer in mates
        ]

    def sum_near(layer):
        total = part_own[layer, mine].astype(F32)
        for i, copy in enumerate(scatter_copies(layer)):
            copy.wait_recv()
            total = total + part_got[layer, i].astype(F32)
        mid[layer, level] = total.astype(BF16)
        for copy in level_copies(layer):
            copy.start()

    def sum_far(layer):
        for copy in level_copies(layer):
            copy.wait_recv()
        total = mid[layer, 0].astype(F32)
        for z in range(1, far_group):
            total = total + mid[layer, z].astype(F32)
        final[layer, mine] = total.astype(BF16)
        for copy in gather_copies(layer):
            copy.start()

    def store(layer):
        return pltpu.make_async_copy(staged.at[layer], grad_out.at[layer], store_sem.at[layer])

    def finish(layer):
        for copy in gather_copies(layer):
            copy.wait_recv()
        whole = jnp.concatenate([final[layer, i] for i in range(near_group)], axis=0)
        for k in range(taps):
            staged[layer, k] = whole[:, k * chans : (k + 1) * chans]
        store(layer).start()

    @pl.when(jnp.logical_not(has_left))
    def _():
        from_side[0] = jnp.zeros(from_side.shape[1:], BF16)
        back_side[0] = jnp.zeros(back_side.shape[1:], BF16)
        got_left[...] = jnp.zeros_like(got_left)

    @pl.when(jnp.logical_not(has_right))
    def _():
        from_side[1] = jnp.zeros(from_side.shape[1:], BF16)
        back_side[1] = jnp.zeros(back_side.shape[1:], BF16)
        got_right[...] = jnp.zeros_like(got_right)

    loads[1].wait()
    loads[2].wait()
    first = (sky - 1) * rows
    near = nb[...]
    offset = jnp.where(near >= 0, near - first, -1)
    part = jnp.where(
        offset < 0, -1,
        jnp.where(offset < rows, offset + rows, jnp.where(offset < 2 * rows, offset - rows, offset)),
    )
    rel[...] = jnp.full(rel.shape, -1, jnp.int32)
    rel[0:taps, :] = part
    col = jnp.transpose(rel[...])
    turned[...] = col
    for k in range(taps):
        lanes = slice(k * rows, (k + 1) * rows)
        line = rel[k : k + 1, :]
        for p in range(3):
            index = lax.broadcasted_iota(jnp.int32, (rows, rows), 0) + p * rows
            one_hot[p * rows : (p + 1) * rows, lanes] = jnp.where(line == index, 1.0, 0.0).astype(BF16)
    pl.semaphore_wait(
        barrier,
        has_left.astype(jnp.int32) + has_right.astype(jnp.int32)
        + (n_branch - 1 + near_group - 1 + far_group - 1),
    )

    loads[0].wait()
    start(halo(0))
    loads[3].wait()
    join_copies = across(join, join_got, 0)
    for copy in join_copies:
        copy.start()

    for load in loads[4:]:
        load.wait()
    retained = foot[...].astype(F32)
    dec_acc[...] = jnp.zeros_like(dec_acc)
    dec_cuts = [0, taps // 9, 4 * taps // 9, 7 * taps // 9, taps]
    dec_steps = len(dec_cuts) - 1

    @pl.loop(0, depth)
    def forward(layer):
        hidden = own[layer]
        for k in range(taps):
            block = matmul(hidden, one_hot[0:rows, k * rows : (k + 1) * rows])
            picked[layer, k * chans : (k + 1) * chans, :] = block.astype(BF16)
        for k in range(taps):
            tap = enc[layer, k]
            enc_flat[layer, :, k * chans : (k + 1) * chans] = tap
            enc_t[layer, :, k * chans : (k + 1) * chans] = jnp.transpose(tap)

        def decode(step):
            low, high = dec_cuts[step], dec_cuts[step + 1]
            parts = []
            for k in range(low, high):
                line = turned[:, k : k + 1]
                for p in range(3):
                    index = lax.broadcasted_iota(jnp.int32, (rows, rows), 1) + p * rows
                    one_hot_t[p, k * rows : (k + 1) * rows, :] = jnp.where(
                        line == index, 1.0, 0.0
                    ).astype(BF16)
                parts.append(matmul(dec[k], cot[...], ((0,), (0,))).astype(BF16))
            terms = jnp.concatenate(parts, axis=1)
            span = slice(low * rows, high * rows)
            for p in range(3):
                dec_acc[p] = dec_acc[p] + matmul(terms, one_hot_t[p, span, :])

        for step in range(dec_steps):
            pl.when(layer == step)(functools.partial(decode, step))

        @pl.when(layer == dec_steps)
        def _():
            rim_left[...] = dec_acc[1].astype(BF16)
            rim_right[...] = dec_acc[2].astype(BF16)
            start(rims())

        @pl.when(layer == dec_steps + 1)
        def _():
            wait_recv(rims())
            total = dec_acc[0] + got_left[...].astype(F32) + got_right[...].astype(F32)
            unit_own[...] = total
            unit_send[...] = total.astype(BF16)
            for copy in across(unit_send, unit_got, 1):
                copy.start()

        for side in (close, distant):
            wait_recv_side(halo(layer), side)
            arrived = from_side[side, layer]
            table = pl.ds(pl.multiple_of((1 + side) * rows, rows), rows)
            for k in range(taps):
                block = matmul(arrived, one_hot[table, k * rows : (k + 1) * rows])
                at = slice(k * chans, (k + 1) * chans)
                picked[layer, at, :] = picked[layer, at, :] + block.astype(BF16)
        pre = matmul(enc_flat[layer], picked[layer])
        sig = jax.nn.sigmoid(pre)
        after = retained * (hidden.astype(F32) + pre * sig)
        own[layer + 1] = after.astype(BF16)

        @pl.when(layer < depth - 1)
        def _():
            start(halo(layer + 1))

        slope[layer] = sig * (1.0 + pre * (1.0 - sig))

    top_copies = across(own.at[depth], top_got, 2)
    for copy in top_copies:
        copy.start()
    joined = matmul(join[...], own[depth], ((0,), (0,)))
    for copy in join_copies:
        copy.wait_recv()
    unit_copies = across(unit_send, unit_got, 1)
    unit = unit_own[...]
    for i, copy in enumerate(unit_copies):
        copy.wait_recv()
        unit = unit + unit_got[i].astype(F32)
    for i, copy in enumerate(top_copies):
        copy.wait_recv()
        joined = joined + matmul(join_got[i], top_got[i], ((0,), (0,)))
    sig = jax.nn.sigmoid(joined)
    unit_slope = (sig * (1.0 + joined * (1.0 - sig))).astype(BF16).astype(F32)
    unit_grad = (unit * unit_slope).astype(BF16)
    grad[...] = matmul(join[...], unit_grad)

    def weigh(layer, act):
        weight = matmul(act, picked[layer], ((1,), (1,)))
        for i in range(near_group):
            part_own[layer, i] = weight[i * share : (i + 1) * share].astype(BF16)
        for copy in scatter_copies(layer):
            copy.start()

    def spread(layer, act):
        def placed(part):
            spots = [
                matmul(act, one_hot_t[part, k * rows : (k + 1) * rows, :]).astype(BF16)
                for k in range(taps)
            ]
            return matmul(enc_t[layer], jnp.concatenate(spots, axis=0))

        for side in (distant, close):
            edge[side, layer] = placed(1 + side).astype(BF16)
            start_side(back(layer), side)
        return placed(0)

    def take_back(layer, inner):
        wait_recv(back(layer))
        return inner + back_side[0, layer].astype(F32) + back_side[1, layer].astype(F32)

    @pl.loop(0, depth - 1)
    def backward(step):
        layer = depth - 1 - step
        masked = retained * grad[...]
        act = (masked * slope[layer]).astype(BF16)
        inner = masked + spread(layer, act)
        weigh(layer, act)

        @pl.when(step >= 1)
        def _():
            sum_near(layer + 1)

        @pl.when(step >= 2)
        def _():
            sum_far(layer + 2)

        @pl.when(step >= 3)
        def _():
            finish(layer + 3)

        grad[...] = take_back(layer, inner)

    masked = retained * grad[...]
    act = (masked * slope[0]).astype(BF16)
    weigh(0, act)
    inner = masked + spread(0, act)
    late = [k for k in (1, 2, 3) if k < depth]
    for k, stage in zip(late, (sum_near, sum_far, finish)):
        stage(k)
    sum_near(0)
    if depth > 1:
        sum_far(1)
    if depth > 2:
        finish(2)
    map_own[...] = take_back(0, inner).astype(BF16)
    map_copy = pltpu.make_async_copy(map_own, map_out, local_sem.at[0])
    map_copy.start()
    sum_far(0)
    if depth > 1:
        finish(1)
    finish(0)
    map_copy.wait()

    @pl.loop(0, depth)
    def drain(layer):
        wait_send(halo(layer))
        wait_send(back(layer))
        store(layer).wait()
        for copy in scatter_copies(layer) + level_copies(layer) + gather_copies(layer):
            copy.wait_send()

    wait_send(rims())
    for copy in join_copies + unit_copies + top_copies:
        copy.wait_send()


def scale_kernel(normalizer, map_in, sums_in, map_out, sums_out, held, sums, scaled, in_sem, out_sem):
    depth = sums_in.shape[0]
    reads = [pltpu.make_async_copy(sums_in.at[i], sums.at[i], in_sem.at[i]) for i in range(depth)]
    writes = [
        pltpu.make_async_copy(scaled.at[i], sums_out.at[i], out_sem.at[i]) for i in range(depth)
    ]
    reads.append(pltpu.make_async_copy(map_in, held, in_sem.at[depth]))
    writes.append(pltpu.make_async_copy(held, map_out, out_sem.at[depth]))
    for read in reads:
        read.start()
    for i in range(depth):
        reads[i].wait()
        scaled[i] = sums[i].astype(F32) * normalizer
        writes[i].start()
    reads[depth].wait()
    writes[depth].start()
    for write in writes:
        write.wait()


def per_device(n_sky, n_branch, sky_maps, footprint, neighbours, enc_weight, join_weight, dec_weight, cotangent):
    chans, rows = sky_maps.shape[1:]
    depth, taps = enc_weight.shape[1:3]
    width = dec_weight.shape[2]
    others = max(n_branch - 1, 1)
    near_group = math.gcd(n_sky, 4)
    far_group = n_sky // near_group
    share = chans // near_group
    near, far = max(near_group - 1, 1), max(far_group - 1, 1)
    vmem = pltpu.VMEM
    dma = pltpu.SemaphoreType.DMA
    layers = (depth, chans, rows)
    scratch = [
        vmem(footprint.shape, jnp.int32),
        vmem(neighbours.shape, jnp.int32),
        vmem(enc_weight.shape[1:], BF16),
        vmem((chans, width), BF16),
        vmem(dec_weight.shape, BF16),
        vmem(cotangent.shape, BF16),
        vmem((depth + 1, chans, rows), BF16),
        vmem((2,) + layers, BF16),
        vmem((depth, taps * chans, rows), BF16),
        vmem(layers, F32),
        vmem((3 * rows, taps * rows), BF16),
        vmem((3, taps * rows, rows), BF16),
        vmem((128, rows), jnp.int32),
        vmem((rows, 128), jnp.int32),
        vmem((depth, chans, taps * chans), BF16),
        vmem((depth, chans, taps * chans), BF16),
        vmem((chans, rows), F32),
        vmem((2,) + layers, BF16),
        vmem((2,) + layers, BF16),
        vmem((depth, taps, chans, chans), BF16),
        vmem((chans, rows), BF16),
        vmem((3, width, rows), F32),
        vmem((width, rows), BF16),
        vmem((width, rows), BF16),
        vmem((width, rows), BF16),
        vmem((width, rows), BF16),
        vmem((width, rows), F32),
        vmem((width, rows), BF16),
        vmem((others, width, rows), BF16),
        vmem((others, chans, width), BF16),
        vmem((others, chans, rows), BF16),
        vmem((depth, near_group, share, taps * chans), BF16),
        vmem((depth, near, share, taps * chans), BF16),
        vmem((depth, far_group, share, taps * chans), BF16),
        vmem((depth, near_group, share, taps * chans), BF16),
        dma((depth, 2)), dma((depth, 2)), dma((depth, 2)), dma((depth, 2)),
        dma((2,)), dma((2,)), dma((3, others)), dma((3, others)),
        dma((depth, near)), dma((depth, near)), dma((depth, far)), dma((depth, far)),
        dma((depth, near)), dma((depth, near)), dma((7,)), dma((depth,)),
    ]
    hbm = pl.BlockSpec(memory_space=pltpu.HBM)
    map_grad, tap_grads = pl.pallas_call(
        functools.partial(kernel, n_sky, n_branch, near_group),
        out_shape=(
            jax.ShapeDtypeStruct((chans, rows), BF16),
            jax.ShapeDtypeStruct((depth, taps, chans, chans), BF16),
        ),
        in_specs=[hbm] * 7,
        out_specs=(hbm, hbm),
        scratch_shapes=scratch,
        compiler_params=pltpu.CompilerParams(
            collective_id=0, has_side_effects=True, vmem_limit_bytes=60 * 1024 * 1024
        ),
        name="unet_backward",
    )(sky_maps[0], footprint, neighbours, enc_weight[0], join_weight.T, dec_weight, cotangent)
    normalizer = 1.0 / math.sqrt(rows * n_sky)
    map_grad, summed = pl.pallas_call(
        functools.partial(scale_kernel, normalizer),
        out_shape=(
            jax.ShapeDtypeStruct((chans, rows), BF16),
            jax.ShapeDtypeStruct((depth, taps, chans, chans), F32),
        ),
        in_specs=[hbm] * 2,
        out_specs=(hbm, hbm),
        scratch_shapes=[
            vmem((chans, rows), BF16),
            vmem((depth, taps, chans, chans), BF16),
            vmem((depth, taps, chans, chans), F32),
            dma((depth + 1,)),
            dma((depth + 1,)),
        ],
        compiler_params=pltpu.CompilerParams(vmem_limit_bytes=60 * 1024 * 1024),
        name="scale_sums",
    )(map_grad, tap_grads)
    return map_grad[None], summed[None]


def solution(mesh):
    in_specs = (
        P("branch", None, "sky"),
        P("branch", "sky"),
        P(None, "sky"),
        P("branch", None, None, None, None),
        P(None, "branch"),
        P(None, "branch", None),
        P("branch", "sky"),
    )
    out_specs = (P("branch", None, "sky"), P("branch", None, None, None, None))
    return jax.shard_map(
        functools.partial(per_device, mesh.shape["sky"], mesh.shape["branch"]),
        mesh=mesh, in_specs=in_specs, out_specs=out_specs, check_vma=False,
    )
```

```python
import functools
import math

import jax
import jax.numpy as jnp
from jax import lax
from jax.experimental import pallas as pl
from jax.experimental.pallas import tpu as pltpu
from jax.sharding import PartitionSpec as P

MESH = pl.DeviceIdType.MESH
F32 = jnp.float32
BF16 = jnp.bfloat16


def matmul(a, b, contract=((1,), (0,))):
    return lax.dot_general(a, b, (contract, ((), ())), preferred_element_type=F32)


def kernel(
    n_sky, n_branch, near_group,
    maps_in, foot_in, nb_in, enc_in, join_in, dec_in, cot_in,
    map_out, grad_out,
    foot, nb, enc, join, dec, cot,
    own, from_side, picked, slope, one_hot, one_hot_t, rel, turned, enc_flat, enc_t,
    grad, edge, back_side, staged, map_own,
    dec_acc, rim_left, rim_right, got_left, got_right, unit_own, unit_send, unit_got,
    join_got, top_got,
    part_own, part_got, mid, final,
    fwd_send, fwd_recv, bwd_send, bwd_recv, rim_send, rim_recv, br_send, br_recv,
    near_send, near_recv, far_send, far_recv, out_send, out_recv, local_sem, store_sem,
):
    depth, taps = enc.shape[0], enc.shape[1]
    chans, rows = maps_in.shape
    far_group = n_sky // near_group
    share = chans // near_group
    sky = lax.axis_index("sky")
    branch = lax.axis_index("branch")
    has_left, has_right = sky > 0, sky < n_sky - 1
    left, right = jnp.maximum(sky - 1, 0), jnp.minimum(sky + 1, n_sky - 1)
    peers = [(d, lax.rem(branch + d, n_branch)) for d in range(1, n_branch)]

    mine = lax.rem(sky, near_group)
    level = sky // near_group
    mates = [
        (d, sky - mine + lax.rem(mine + d, near_group)) for d in range(1, near_group)
    ]
    stack = [
        (d, lax.rem(level + d, far_group) * near_group + mine) for d in range(1, far_group)
    ]

    sources = (maps_in, foot_in, nb_in, join_in, enc_in, dec_in, cot_in)
    targets = (own.at[0], foot, nb, join, enc, dec, cot)
    loads = [
        pltpu.make_async_copy(src, dst, local_sem.at[i])
        for i, (src, dst) in enumerate(zip(sources, targets))
    ]
    for load in loads:
        load.start()

    barrier = pltpu.get_barrier_semaphore()

    @pl.when(has_left)
    def _():
        pl.semaphore_signal(barrier, inc=1, device_id={"sky": left}, device_id_type=MESH)

    @pl.when(has_right)
    def _():
        pl.semaphore_signal(barrier, inc=1, device_id={"sky": right}, device_id_type=MESH)

    for _, peer in peers:
        pl.semaphore_signal(barrier, inc=1, device_id={"branch": peer}, device_id_type=MESH)
    for _, peer in mates + stack:
        pl.semaphore_signal(barrier, inc=1, device_id={"sky": peer}, device_id_type=MESH)
    def to_left(src, dst, send, recv):
        return pltpu.make_async_remote_copy(
            src_ref=src, dst_ref=dst, send_sem=send, recv_sem=recv,
            device_id={"sky": left}, device_id_type=MESH,
        )

    def to_right(src, dst, send, recv):
        return pltpu.make_async_remote_copy(
            src_ref=src, dst_ref=dst, send_sem=send, recv_sem=recv,
            device_id={"sky": right}, device_id_type=MESH,
        )

    def halo(layer):
        return (
            to_left(own.at[layer], from_side.at[1, layer], fwd_send.at[layer, 0], fwd_recv.at[layer, 0]),
            to_right(own.at[layer], from_side.at[0, layer], fwd_send.at[layer, 1], fwd_recv.at[layer, 1]),
        )

    def back(layer):
        return (
            to_left(edge.at[0, layer], back_side.at[1, layer], bwd_send.at[layer, 0], bwd_recv.at[layer, 0]),
            to_right(edge.at[1, layer], back_side.at[0, layer], bwd_send.at[layer, 1], bwd_recv.at[layer, 1]),
        )

    def rims():
        return (
            to_left(rim_left, got_right, rim_send.at[0], rim_recv.at[0]),
            to_right(rim_right, got_left, rim_send.at[1], rim_recv.at[1]),
        )

    def start(pair):
        @pl.when(has_left)
        def _():
            pair[0].start()

        @pl.when(has_right)
        def _():
            pair[1].start()

    def wait_recv(pair):
        @pl.when(has_right)
        def _():
            pair[0].wait_recv()

        @pl.when(has_left)
        def _():
            pair[1].wait_recv()

    def wait_recv_side(pair, side):
        @pl.when(jnp.logical_and(side == 1, has_right))
        def _():
            pair[0].wait_recv()

        @pl.when(jnp.logical_and(side == 0, has_left))
        def _():
            pair[1].wait_recv()

    def start_side(pair, side):
        @pl.when(jnp.logical_and(side == 0, has_left))
        def _():
            pair[0].start()

        @pl.when(jnp.logical_and(side == 1, has_right))
        def _():
            pair[1].start()

    close = 1 - lax.rem(sky, 2)
    distant = 1 - close

    def wait_send(pair):
        @pl.when(has_left)
        def _():
            pair[0].wait_send()

        @pl.when(has_right)
        def _():
            pair[1].wait_send()

    def across(src, dst, kind):
        return [
            pltpu.make_async_remote_copy(
                src_ref=src, dst_ref=dst.at[d - 1],
                send_sem=br_send.at[kind, d - 1], recv_sem=br_recv.at[kind, d - 1],
                device_id={"branch": peer}, device_id_type=MESH,
            )
            for d, peer in peers
        ]

    def over_sky(peer, src, dst, send, recv):
        return pltpu.make_async_remote_copy(
            src_ref=src, dst_ref=dst, send_sem=send, recv_sem=recv,
            device_id={"sky": peer}, device_id_type=MESH,
        )

    def scatter_copies(layer):
        return [
            over_sky(
                peer, part_own.at[layer, lax.rem(mine + d, near_group)], part_got.at[layer, d - 1],
                near_send.at[layer, d - 1], near_recv.at[layer, d - 1],
            )
            for d, peer in mates
        ]

    def level_copies(layer):
        return [
            over_sky(
                peer, mid.at[layer, level], mid.at[layer, level],
                far_send.at[layer, d - 1], far_recv.at[layer, d - 1],
            )
            for d, peer in stack
        ]

    def gather_copies(layer):
        return [
            over_sky(
                peer, final.at[layer, mine], final.at[layer, mine],
                out_send.at[layer, d - 1], out_recv.at[layer, d - 1],
            )
            for d, peer in mates
        ]

    def sum_near(layer):
        total = part_own[layer, mine].astype(F32)
        for i, copy in enumerate(scatter_copies(layer)):
            copy.wait_recv()
            total = total + part_got[layer, i].astype(F32)
        mid[layer, level] = total.astype(BF16)
        for copy in level_copies(layer):
            copy.start()

    def sum_far(layer):
        for copy in level_copies(layer):
            copy.wait_recv()
        total = mid[layer, 0].astype(F32)
        for z in range(1, far_group):
            total = total + mid[layer, z].astype(F32)
        final[layer, mine] = total.astype(BF16)
        for copy in gather_copies(layer):
            copy.start()

    def store(layer):
        return pltpu.make_async_copy(staged.at[layer], grad_out.at[layer], store_sem.at[layer])

    def finish(layer):
        for copy in gather_copies(layer):
            copy.wait_recv()
        whole = jnp.concatenate([final[layer, i] for i in range(near_group)], axis=0)
        for k in range(taps):
            staged[layer, k] = whole[:, k * chans : (k + 1) * chans]
        store(layer).start()

    @pl.when(jnp.logical_not(has_left))
    def _():
        from_side[0] = jnp.zeros(from_side.shape[1:], BF16)
        back_side[0] = jnp.zeros(back_side.shape[1:], BF16)
        got_left[...] = jnp.zeros_like(got_left)

    @pl.when(jnp.logical_not(has_right))
    def _():
        from_side[1] = jnp.zeros(from_side.shape[1:], BF16)
        back_side[1] = jnp.zeros(back_side.shape[1:], BF16)
        got_right[...] = jnp.zeros_like(got_right)

    loads[1].wait()
    loads[2].wait()
    first = (sky - 1) * rows
    near = nb[...]
    offset = jnp.where(near >= 0, near - first, -1)
    part = jnp.where(
        offset < 0, -1,
        jnp.where(offset < rows, offset + rows, jnp.where(offset < 2 * rows, offset - rows, offset)),
    )
    rel[...] = jnp.full(rel.shape, -1, jnp.int32)
    rel[0:taps, :] = part
    col = jnp.transpose(rel[...])
    turned[...] = col
    for k in range(taps):
        lanes = slice(k * rows, (k + 1) * rows)
        line = rel[k : k + 1, :]
        for p in range(3):
            index = lax.broadcasted_iota(jnp.int32, (rows, rows), 0) + p * rows
            one_hot[p * rows : (p + 1) * rows, lanes] = jnp.where(line == index, 1.0, 0.0).astype(BF16)
    pl.semaphore_wait(
        barrier,
        has_left.astype(jnp.int32) + has_right.astype(jnp.int32)
        + (n_branch - 1 + near_group - 1 + far_group - 1),
    )

    loads[0].wait()
    start(halo(0))
    loads[3].wait()
    join_copies = across(join, join_got, 0)
    for copy in join_copies:
        copy.start()

    for load in loads[4:]:
        load.wait()
    retained = foot[...].astype(F32)
    dec_acc[...] = jnp.zeros_like(dec_acc)
    dec_cuts = [0, taps // 9, 4 * taps // 9, 7 * taps // 9, taps]
    dec_steps = len(dec_cuts) - 1

    @pl.loop(0, depth)
    def forward(layer):
        hidden = own[layer]
        for k in range(taps):
            block = matmul(hidden, one_hot[0:rows, k * rows : (k + 1) * rows])
            picked[layer, k * chans : (k + 1) * chans, :] = block.astype(BF16)
        for k in range(taps):
            tap = enc[layer, k]
            enc_flat[layer, :, k * chans : (k + 1) * chans] = tap
            enc_t[layer, k * chans : (k + 1) * chans, :] = jnp.transpose(tap)

        def decode(step):
            low, high = dec_cuts[step], dec_cuts[step + 1]
            parts = []
            for k in range(low, high):
                line = turned[:, k : k + 1]
                for p in range(3):
                    index = lax.broadcasted_iota(jnp.int32, (rows, rows), 1) + p * rows
                    one_hot_t[p, k * rows : (k + 1) * rows, :] = jnp.where(
                        line == index, 1.0, 0.0
                    ).astype(BF16)
                parts.append(matmul(dec[k], cot[...], ((0,), (0,))).astype(BF16))
            terms = jnp.concatenate(parts, axis=1)
            span = slice(low * rows, high * rows)
            for p in range(3):
                dec_acc[p] = dec_acc[p] + matmul(terms, one_hot_t[p, span, :])

        for step in range(dec_steps):
            pl.when(layer == step)(functools.partial(decode, step))

        @pl.when(layer == dec_steps)
        def _():
            rim_left[...] = dec_acc[1].astype(BF16)
            rim_right[...] = dec_acc[2].astype(BF16)
            start(rims())

        @pl.when(layer == dec_steps + 1)
        def _():
            wait_recv(rims())
            total = dec_acc[0] + got_left[...].astype(F32) + got_right[...].astype(F32)
            unit_own[...] = total
            unit_send[...] = total.astype(BF16)
            for copy in across(unit_send, unit_got, 1):
                copy.start()

        for side in (close, distant):
            wait_recv_side(halo(layer), side)
            arrived = from_side[side, layer]
            table = pl.ds(pl.multiple_of((1 + side) * rows, rows), rows)
            for k in range(taps):
                block = matmul(arrived, one_hot[table, k * rows : (k + 1) * rows])
                at = slice(k * chans, (k + 1) * chans)
                picked[layer, at, :] = picked[layer, at, :] + block.astype(BF16)
        pre = matmul(enc_flat[layer], picked[layer])
        sig = jax.nn.sigmoid(pre)
        after = retained * (hidden.astype(F32) + pre * sig)
        own[layer + 1] = after.astype(BF16)

        @pl.when(layer < depth - 1)
        def _():
            for side in (distant, close):
                start_side(halo(layer + 1), side)

        slope[layer] = sig * (1.0 + pre * (1.0 - sig))

    top_copies = across(own.at[depth], top_got, 2)
    for copy in top_copies:
        copy.start()
    joined = matmul(join[...], own[depth], ((0,), (0,)))
    for copy in join_copies:
        copy.wait_recv()
    unit_copies = across(unit_send, unit_got, 1)
    unit = unit_own[...]
    for i, copy in enumerate(unit_copies):
        copy.wait_recv()
        unit = unit + unit_got[i].astype(F32)
    for i, copy in enumerate(top_copies):
        copy.wait_recv()
        joined = joined + matmul(join_got[i], top_got[i], ((0,), (0,)))
    sig = jax.nn.sigmoid(joined)
    unit_slope = (sig * (1.0 + joined * (1.0 - sig))).astype(BF16).astype(F32)
    unit_grad = (unit * unit_slope).astype(BF16)
    grad[...] = matmul(join[...], unit_grad)

    def weigh(layer, act):
        weight = matmul(act, picked[layer], ((1,), (1,)))
        for i in range(near_group):
            part_own[layer, i] = weight[i * share : (i + 1) * share].astype(BF16)
        for copy in scatter_copies(layer):
            copy.start()

    def spread(layer, act):
        terms = matmul(enc_t[layer], act).astype(BF16)
        terms = jnp.concatenate(
            [terms[k * chans : (k + 1) * chans] for k in range(taps)], axis=1
        )
        for side in (distant, close):
            edge[side, layer] = matmul(terms, one_hot_t[1 + side]).astype(BF16)
            start_side(back(layer), side)
        return matmul(terms, one_hot_t[0])

    def take_back(layer, inner):
        wait_recv(back(layer))
        return inner + back_side[0, layer].astype(F32) + back_side[1, layer].astype(F32)

    @pl.loop(0, depth - 1)
    def backward(step):
        layer = depth - 1 - step
        masked = retained * grad[...]
        act = (masked * slope[layer]).astype(BF16)
        inner = masked + spread(layer, act)
        weigh(layer, act)

        @pl.when(step >= 1)
        def _():
            sum_near(layer + 1)

        @pl.when(step >= 2)
        def _():
            sum_far(layer + 2)

        @pl.when(step >= 3)
        def _():
            finish(layer + 3)

        grad[...] = take_back(layer, inner)

    masked = retained * grad[...]
    act = (masked * slope[0]).astype(BF16)
    weigh(0, act)
    inner = masked + spread(0, act)
    late = [k for k in (1, 2, 3) if k < depth]
    for k, stage in zip(late, (sum_near, sum_far, finish)):
        stage(k)
    sum_near(0)
    if depth > 1:
        sum_far(1)
    if depth > 2:
        finish(2)
    map_own[...] = take_back(0, inner).astype(BF16)
    map_copy = pltpu.make_async_copy(map_own, map_out, local_sem.at[0])
    map_copy.start()
    sum_far(0)
    if depth > 1:
        finish(1)
    finish(0)
    map_copy.wait()

    @pl.loop(0, depth)
    def drain(layer):
        wait_send(halo(layer))
        wait_send(back(layer))
        store(layer).wait()
        for copy in scatter_copies(layer) + level_copies(layer) + gather_copies(layer):
            copy.wait_send()

    wait_send(rims())
    for copy in join_copies + unit_copies + top_copies:
        copy.wait_send()


def scale_kernel(normalizer, map_in, sums_in, map_out, sums_out, held, sums, scaled, in_sem, out_sem):
    depth = sums_in.shape[0]
    reads = [pltpu.make_async_copy(sums_in.at[i], sums.at[i], in_sem.at[i]) for i in range(depth)]
    writes = [
        pltpu.make_async_copy(scaled.at[i], sums_out.at[i], out_sem.at[i]) for i in range(depth)
    ]
    reads.append(pltpu.make_async_copy(map_in, held, in_sem.at[depth]))
    writes.append(pltpu.make_async_copy(held, map_out, out_sem.at[depth]))
    for read in reads:
        read.start()
    for i in range(depth):
        reads[i].wait()
        scaled[i] = sums[i].astype(F32) * normalizer
        writes[i].start()
    reads[depth].wait()
    writes[depth].start()
    for write in writes:
        write.wait()


def per_device(n_sky, n_branch, sky_maps, footprint, neighbours, enc_weight, join_weight, dec_weight, cotangent):
    chans, rows = sky_maps.shape[1:]
    depth, taps = enc_weight.shape[1:3]
    width = dec_weight.shape[2]
    others = max(n_branch - 1, 1)
    near_group = math.gcd(n_sky, 4)
    far_group = n_sky // near_group
    share = chans // near_group
    near, far = max(near_group - 1, 1), max(far_group - 1, 1)
    vmem = pltpu.VMEM
    dma = pltpu.SemaphoreType.DMA
    layers = (depth, chans, rows)
    scratch = [
        vmem(footprint.shape, jnp.int32),
        vmem(neighbours.shape, jnp.int32),
        vmem(enc_weight.shape[1:], BF16),
        vmem((chans, width), BF16),
        vmem(dec_weight.shape, BF16),
        vmem(cotangent.shape, BF16),
        vmem((depth + 1, chans, rows), BF16),
        vmem((2,) + layers, BF16),
        vmem((depth, taps * chans, rows), BF16),
        vmem(layers, F32),
        vmem((3 * rows, taps * rows), BF16),
        vmem((3, taps * rows, rows), BF16),
        vmem((128, rows), jnp.int32),
        vmem((rows, 128), jnp.int32),
        vmem((depth, chans, taps * chans), BF16),
        vmem((depth, taps * chans, chans), BF16),
        vmem((chans, rows), F32),
        vmem((2,) + layers, BF16),
        vmem((2,) + layers, BF16),
        vmem((depth, taps, chans, chans), BF16),
        vmem((chans, rows), BF16),
        vmem((3, width, rows), F32),
        vmem((width, rows), BF16),
        vmem((width, rows), BF16),
        vmem((width, rows), BF16),
        vmem((width, rows), BF16),
        vmem((width, rows), F32),
        vmem((width, rows), BF16),
        vmem((others, width, rows), BF16),
        vmem((others, chans, width), BF16),
        vmem((others, chans, rows), BF16),
        vmem((depth, near_group, share, taps * chans), BF16),
        vmem((depth, near, share, taps * chans), BF16),
        vmem((depth, far_group, share, taps * chans), BF16),
        vmem((depth, near_group, share, taps * chans), BF16),
        dma((depth, 2)), dma((depth, 2)), dma((depth, 2)), dma((depth, 2)),
        dma((2,)), dma((2,)), dma((3, others)), dma((3, others)),
        dma((depth, near)), dma((depth, near)), dma((depth, far)), dma((depth, far)),
        dma((depth, near)), dma((depth, near)), dma((7,)), dma((depth,)),
    ]
    hbm = pl.BlockSpec(memory_space=pltpu.HBM)
    map_grad, tap_grads = pl.pallas_call(
        functools.partial(kernel, n_sky, n_branch, near_group),
        out_shape=(
            jax.ShapeDtypeStruct((chans, rows), BF16),
            jax.ShapeDtypeStruct((depth, taps, chans, chans), BF16),
        ),
        in_specs=[hbm] * 7,
        out_specs=(hbm, hbm),
        scratch_shapes=scratch,
        compiler_params=pltpu.CompilerParams(
            collective_id=0, has_side_effects=True, vmem_limit_bytes=60 * 1024 * 1024
        ),
        name="unet_backward",
    )(sky_maps[0], footprint, neighbours, enc_weight[0], join_weight.T, dec_weight, cotangent)
    normalizer = 1.0 / math.sqrt(rows * n_sky)
    map_grad, summed = pl.pallas_call(
        functools.partial(scale_kernel, normalizer),
        out_shape=(
            jax.ShapeDtypeStruct((chans, rows), BF16),
            jax.ShapeDtypeStruct((depth, taps, chans, chans), F32),
        ),
        in_specs=[hbm] * 2,
        out_specs=(hbm, hbm),
        scratch_shapes=[
            vmem((chans, rows), BF16),
            vmem((depth, taps, chans, chans), BF16),
            vmem((depth, taps, chans, chans), F32),
            dma((depth + 1,)),
            dma((depth + 1,)),
        ],
        compiler_params=pltpu.CompilerParams(vmem_limit_bytes=60 * 1024 * 1024),
        name="scale_sums",
    )(map_grad, tap_grads)
    return map_grad[None], summed[None]


def solution(mesh):
    in_specs = (
        P("branch", None, "sky"),
        P("branch", "sky"),
        P(None, "sky"),
        P("branch", None, None, None, None),
        P(None, "branch"),
        P(None, "branch", None),
        P("branch", "sky"),
    )
    out_specs = (P("branch", None, "sky"), P("branch", None, None, None, None))
    return jax.shard_map(
        functools.partial(per_device, mesh.shape["sky"], mesh.shape["branch"]),
        mesh=mesh, in_specs=in_specs, out_specs=out_specs, check_vma=False,
    )
```
